256 devices in a mesh: ka: 16 (over z, y_lo), pb: 16 (over y_hi, x, core).
Axes of the slice: x: 4, y: 4 (y_hi: 2, y_lo: 2; y = y_hi * 2 + y_lo), z: 8, core: 2. Of those that a mesh axis runs over, the one named last changes fastest.
Arguments:
- dipole: float32 [16, 4096], P('ka', 'pb'), may hold values from -400 to 400
- energy: float32 [16, 4096], P('ka', 'pb'), may hold values from 1 to 4
- cond_amp: bfloat16 [16, 64, 2048], P('ka', None, 'pb'), may hold values from -6 to 6
- val_amp: bfloat16 [16, 64, 2048], P('pb', None, 'ka'), may hold values from -6 to 6
- screened: bfloat16 [128, 2048, 2048], P('pb', None, 'ka'), may hold values from -6 to 6
- window: int32 [16], replicated, may hold values from 0 to 127, as said below
Outputs:
- coefficients: float32 [4], replicated
- last_vector: float32 [16, 4096], P('ka', 'pb')
The draws below stay inside these ranges and needn't reach their ends.
Inputs may be any that keep to these rules, and one draw needn't show every extreme that they name: `window`: distinct grid indices; the first two are 0 and 127.
All inputs are finite; a program needn't handle non-finite values.
Results may differ from the reference program's by a relative error of at most 0.018.
Values may be sent and summed in bfloat16 or wider, within the bound.
A program may use at most 64 MiB of HBM per device.

```python
import math
import jax
import jax.numpy as jnp
from jax import lax

NC = 64
NV = 64
NG = 2048
ITERS = 2
GX = 4
GY = 8
NK = 16
NQ = 128
NCV = 4096


def draw_window(key, part):
    key = jax.random.fold_in(key, 7)
    shuffled = jax.random.permutation(key, NQ - 2) + 1
    corners = jnp.array([0, NQ - 1], jnp.int32)
    return jnp.concatenate([corners, shuffled[:NK - 2].astype(jnp.int32)])


def draw_dipole(key, part):
    key = jax.random.fold_in(key, 11)
    key_vals, key_rows, key_cols = jax.random.split(key, 3)
    k_ramp = jnp.exp(math.log(3.0) * jnp.arange(NK, dtype=jnp.float32) / max(NK - 1, 1))
    row_scale = k_ramp * jnp.exp(jax.random.uniform(key_rows, (NK,), jnp.float32, 0.0, math.log(3.3)))
    col_scale = jnp.exp(jax.random.uniform(key_cols, (NC * NV,), jnp.float32, 0.0, math.log(10.0)))
    values = jnp.clip(jax.random.normal(key_vals, (NK, NC * NV), jnp.float32), -4.0, 4.0)
    return values * row_scale[:, None] * col_scale[None, :]


def level_of(own_key, shape, cuts, smallest, high):
    def one(axis_at, blocks):
        steps = jax.random.uniform(jax.random.fold_in(jax.random.fold_in(own_key, 6), axis_at), (blocks,), jnp.float32, smallest / len(cuts), high / len(cuts))
        return jnp.repeat(jnp.exp(steps), shape[axis_at] // blocks).reshape((-1,) + (1,) * (len(shape) - axis_at - 1))

    level = one(*cuts[0])
    for cut in cuts[1:]:
        level = level * one(*cut)
    return level


def bell_draw(own_key, extent, width, bound, pieces=(), kind=jnp.bfloat16):
    entries = jax.random.normal(own_key, extent, jnp.float32) * width
    if len(pieces) > 0:
        entries = level_of(own_key, extent, pieces, -0.22, 0.18) * entries
    return jnp.clip(entries, min=-bound, max=bound).astype(kind)


def setup_inputs(seed: int = 0) -> dict:
    key_list = jax.random.split(jax.random.key(seed), 7)
    return {
        "dipole": draw_dipole(jax.random.fold_in(key_list[6], 71), 0),
        "energy": jnp.clip(1.0 + 3.0 * jax.random.uniform(key_list[1], (NK, NCV), jnp.float32) ** level_of(key_list[1], (NK, NCV), ((0, 16), (1, 16)), -0.2, 0.2), 1.0, 4.0),
        "cond_amp": bell_draw(key_list[2], (NK, NC, NG), 1.0, 6.0, ((0, 16), (2, 16))),
        "val_amp": bell_draw(key_list[3], (NK, NV, NG), 1.0, 6.0, ((0, 16), (2, 16))),
        "screened": bell_draw(key_list[4], (NQ, NG, NG), 1.0, 6.0, ((0, 16), (2, 16))),
        "window": draw_window(jax.random.fold_in(key_list[6], 71), 0),
    }


EPSILON = 1e-06

def q_table(window, q_count):
    third_len = q_count // (GX * GY)
    coord_one = window // (GY * third_len)
    coord_two = window // third_len % GY
    coord_three = window % third_len
    shift_one = jnp.remainder(coord_one[:, None] - coord_one[None, :], GX)
    shift_two = jnp.remainder(coord_two[:, None] - coord_two[None, :], GY)
    shift_three = jnp.remainder(coord_three[:, None] - coord_three[None, :], third_len)
    return ((shift_one * GY + shift_two) * third_len + shift_three).astype(jnp.int32)

def kernel_apply(vector, cond_amp, val_amp, screened, q_index):
    point_count = vector.shape[0]
    vec_half = lax.optimization_barrier(vector.astype(jnp.bfloat16)).astype(jnp.float32)
    vec_half = vec_half.reshape(point_count, NC, NV)
    half_prod = jnp.einsum('kcv,kvh->kch', vec_half, val_amp.astype(jnp.float32), precision=lax.Precision.HIGHEST).astype(jnp.bfloat16)
    half_prod = lax.optimization_barrier(half_prod).astype(jnp.float32)
    pair_dens = jnp.einsum('kcg,kch->kgh', cond_amp.astype(jnp.float32), half_prod, precision=lax.Precision.HIGHEST).astype(jnp.bfloat16)

    def per_point(inputs):
        q_row, cond_row, val_row = inputs

        def accumulate(pair_index, running):
            return running + screened[q_row[pair_index]].astype(jnp.float32) * pair_dens[pair_index].astype(jnp.float32)
        summed = lax.fori_loop(0, point_count, accumulate, jnp.zeros((NG, NG), jnp.float32)).astype(jnp.bfloat16)
        projected = jnp.dot(summed, val_row.T, preferred_element_type=jnp.float32)
        result = jnp.dot(cond_row.astype(jnp.float32), projected, precision=lax.Precision.HIGHEST)
        return result.reshape(NC * NV)
    return lax.map(per_point, (q_index, cond_amp, val_amp))

def reference(dipole, energy, cond_amp, val_amp, screened, window):
    q_index = q_table(window, NQ)
    factor = 1.0 / (NG * math.sqrt(NK * NC * NV))
    vector = dipole / jnp.sqrt(jnp.mean(dipole * dipole) + EPSILON)
    former = jnp.zeros_like(vector)
    beta_now = jnp.zeros((), jnp.float32)
    alpha_list = []
    beta_list = []
    for iteration in range(ITERS):
        kernel_out = kernel_apply(vector, cond_amp, val_amp, screened, q_index)
        image_vec = energy * vector - factor * kernel_out
        alpha_now = jnp.mean(vector * image_vec)
        residual = image_vec - alpha_now * vector - beta_now * former
        beta_now = jnp.sqrt(jnp.mean(residual * residual) + EPSILON)
        former = vector
        vector = residual / beta_now
        alpha_list.append(alpha_now)
        beta_list.append(beta_now)
    coefficients = jnp.stack(alpha_list + beta_list)
    return (coefficients, vector)
```

```python
import functools
import math

import jax
import jax.numpy as jnp
from jax import lax
from jax.experimental import pallas as pl
from jax.experimental.pallas import tpu as pltpu
from jax.sharding import PartitionSpec as P

GX = 4
GY = 8
EPSILON = 1e-06
F32 = jnp.float32
BF16 = jnp.bfloat16
N = 16
VMEM_LIMIT = 48 * 1024 * 1024


def q_table(window, q_count):
    third_len = q_count // (GX * GY)
    coord_one = window // (GY * third_len)
    coord_two = window // third_len % GY
    coord_three = window % third_len
    shift_one = jnp.remainder(coord_one[:, None] - coord_one[None, :], GX)
    shift_two = jnp.remainder(coord_two[:, None] - coord_two[None, :], GY)
    shift_three = jnp.remainder(coord_three[:, None] - coord_three[None, :], third_len)
    return (shift_one * GY + shift_two) * third_len + shift_three


def pair_lists(window):
    chip = lax.axis_index("pb") // 2
    table = q_table(window, 128)
    local = table // 16 == chip
    column = jnp.arange(16, dtype=jnp.int32)
    code = table % 16 * 16 + column[None, :]
    before = jnp.sum(
        (local[:, None, :] & (column[None, None, :] < column[None, :, None])).astype(jnp.int32), axis=2
    )
    hit = local[:, None, :] & (before[:, None, :] == column[None, :, None])
    codes = jnp.sum(jnp.where(hit, code[:, None, :], 0), axis=2)
    counts = jnp.sum(local.astype(jnp.int32), axis=1)
    return codes, counts


def ring_peers(me):
    return [lax.rem(me + o, N) for o in range(1, N)]


def barrier_all(ka, pb):
    barrier = pltpu.get_barrier_semaphore()
    for peer in ring_peers(ka):
        pl.semaphore_signal(barrier, inc=1, device_id={"ka": peer}, device_id_type=pl.DeviceIdType.MESH)
    for peer in ring_peers(pb):
        pl.semaphore_signal(barrier, inc=1, device_id={"pb": peer}, device_id_type=pl.DeviceIdType.MESH)
    pl.semaphore_wait(barrier, 2 * (N - 1))


def send_all(axis, me, source, target, send_sem, recv_sem):
    copies = []
    for o, peer in enumerate(ring_peers(me)):
        copy = pltpu.make_async_remote_copy(
            src_ref=source(peer),
            dst_ref=target(me),
            send_sem=send_sem.at[o],
            recv_sem=recv_sem.at[me],
            device_id={axis: peer},
            device_id_type=pl.DeviceIdType.MESH,
        )
        copy.start()
        copies.append(copy)
    return copies


def recv_all(axis, me, target, send_sem, recv_sem):
    for o, peer in enumerate(ring_peers(me)):
        pltpu.make_async_remote_copy(
            src_ref=target(peer),
            dst_ref=target(peer),
            send_sem=send_sem.at[o],
            recv_sem=recv_sem.at[peer],
            device_id={axis: peer},
            device_id_type=pl.DeviceIdType.MESH,
        ).wait_recv()


def total(x):
    while x.ndim > 2:
        x = jnp.sum(x, axis=0)
    return jnp.sum(jnp.sum(x, axis=0, keepdims=True), axis=1, keepdims=True)


def stat_rows(values):
    row = lax.broadcasted_iota(jnp.int32, (16, 128), 0)
    block = jnp.zeros((16, 128), F32)
    for i, value in enumerate(values):
        rest = jnp.broadcast_to(value, (16, 128))
        for part in range(3):
            piece = rest.astype(BF16).astype(F32)
            block = jnp.where(row == 3 * i + part, piece, block)
            rest = rest - piece
    return block.astype(BF16)


def read_stat(block, i):
    return block[:, 3 * i : 3 * i + 1] + block[:, 3 * i + 1 : 3 * i + 2] + block[:, 3 * i + 2 : 3 * i + 3]


def gather_kernel(
    dip_ref, cond_ref, val_ref, w_ref,
    cond_out, val_out, w_out, row_out, dip_out,
    perm_ref, flat_ref, msg_ref,
    cond_s, cond_r, cpb_s, cpb_r, val_s, val_r, row_s, row_r, dip_s, dip_r, w_sem, own_sem,
):
    ka = lax.axis_index("ka")
    pb = lax.axis_index("pb")
    core = lax.rem(pb, 2)
    block = pb // 2
    to = lax.broadcasted_iota(jnp.int32, (64, 64), 0)
    fro = lax.broadcasted_iota(jnp.int32, (64, 64), 1)
    pick = (fro == 2 * lax.rem(to, 32) + to // 32).astype(F32).astype(BF16)
    perm_ref[...] = jnp.dot(pick, cond_ref[...], preferred_element_type=F32).astype(BF16)
    row_out[pb] = dip_ref[...]
    barrier_all(ka, pb)

    w_copy = pltpu.make_async_remote_copy(
        src_ref=w_ref.at[:, :, 1 - core],
        dst_ref=w_out.at[pl.ds(core * 8, 8)],
        send_sem=w_sem.at[0],
        recv_sem=w_sem.at[1],
        device_id={"pb": pb + 1 - 2 * core},
        device_id_type=pl.DeviceIdType.MESH,
    )
    row_c = send_all("pb", pb, lambda p: dip_ref, lambda p: row_out.at[p], row_s, row_r)
    cond_c = send_all("ka", ka, lambda p: perm_ref, lambda p: cond_out.at[block, p], cond_s, cond_r)
    w_copy.start()
    val_c = send_all("pb", pb, lambda p: val_ref, lambda p: val_out.at[p], val_s, val_r)
    own_cond = pltpu.make_async_copy(perm_ref, cond_out.at[block, ka], own_sem.at[0])
    own_cond.start()
    own_val = pltpu.make_async_copy(val_ref, val_out.at[pb], own_sem.at[1])
    own_val.start()
    own_w = pltpu.make_async_copy(w_ref.at[:, :, core], w_out.at[pl.ds(core * 8, 8)], own_sem.at[2])

    recv_all("pb", pb, lambda p: row_out.at[p], row_s, row_r)
    row = row_out[...]
    square = total(row * row)
    for i in range(N):
        flat_ref[2 * i : 2 * i + 2, :] = row_out[i]
    msg_ref[0:32, :] = flat_ref[...].astype(BF16)
    msg_ref[32:48, :] = stat_rows([square])
    dip_out[ka] = msg_ref[...]
    dip_c = send_all("ka", ka, lambda p: msg_ref, lambda p: dip_out.at[p], dip_s, dip_r)

    own_cond.wait()
    recv_all("ka", ka, lambda p: cond_out.at[block, p], cond_s, cond_r)
    cpb_c = []
    for o in range(1, 8):
        chip = lax.rem(block + o, 8)
        copy = pltpu.make_async_remote_copy(
            src_ref=cond_out.at[block],
            dst_ref=cond_out.at[block],
            send_sem=cpb_s.at[o],
            recv_sem=cpb_r.at[block],
            device_id={"pb": chip * 2 + core},
            device_id_type=pl.DeviceIdType.MESH,
        )
        copy.start()
        cpb_c.append(copy)
    own_w.start()
    recv_all("ka", ka, lambda p: dip_out.at[p], dip_s, dip_r)
    recv_all("pb", pb, lambda p: val_out.at[p], val_s, val_r)
    for o in range(1, 8):
        chip = lax.rem(block + o, 8)
        pltpu.make_async_remote_copy(
            src_ref=cond_out.at[chip],
            dst_ref=cond_out.at[chip],
            send_sem=cpb_s.at[o],
            recv_sem=cpb_r.at[chip],
            device_id={"pb": chip * 2 + core},
            device_id_type=pl.DeviceIdType.MESH,
        ).wait_recv()
    own_val.wait()
    own_w.wait()
    w_copy.wait_send()
    pltpu.make_async_remote_copy(
        src_ref=w_out.at[pl.ds((1 - core) * 8, 8)],
        dst_ref=w_out.at[pl.ds((1 - core) * 8, 8)],
        send_sem=w_sem.at[0],
        recv_sem=w_sem.at[1],
        device_id={"pb": pb + 1 - 2 * core},
        device_id_type=pl.DeviceIdType.MESH,
    ).wait_recv()
    for copy in row_c + cond_c + val_c + dip_c + cpb_c:
        copy.wait_send()


def gather(dipole, cond, val, w):
    sem = pltpu.SemaphoreType.DMA
    vmem = pl.BlockSpec(memory_space=pltpu.VMEM)
    anywhere = pl.BlockSpec(memory_space=pl.ANY)
    return pl.pallas_call(
        gather_kernel,
        out_shape=[
            jax.ShapeDtypeStruct((8, N, 64, 128), BF16),
            jax.ShapeDtypeStruct((N, 64, 128), BF16),
            jax.ShapeDtypeStruct((16, 8, 128, 128), BF16),
            jax.ShapeDtypeStruct((N, 2, 128), F32),
            jax.ShapeDtypeStruct((N, 48, 128), BF16),
        ],
        in_specs=[vmem, vmem, vmem, anywhere],
        out_specs=[anywhere, anywhere, anywhere, vmem, vmem],
        scratch_shapes=[
            pltpu.VMEM((64, 128), BF16),
            pltpu.VMEM((32, 128), F32),
            pltpu.VMEM((48, 128), BF16),
        ]
        + [sem((16,))] * 10
        + [sem((2,)), sem((3,))],
        compiler_params=pltpu.CompilerParams(
            collective_id=0, has_side_effects=True, vmem_limit_bytes=VMEM_LIMIT
        ),
        name="gather",
    )(dipole, cond, val, w)


def two_by_two(val):
    zero = jnp.zeros_like(val)
    return jnp.concatenate(
        [jnp.concatenate([val, zero], axis=1), jnp.concatenate([zero, val], axis=1)], axis=0
    )


def apply_kernel(codes, counts, u_ref, val_ref, cond_ref, w_ref, out_ref, half_ref, pair_ref, sum_ref):
    step = pl.program_id(0)

    @pl.when(step == 0)
    def _():
        sum_ref[...] = jnp.zeros_like(sum_ref)
        for k in range(N):
            both = jnp.dot(u_ref[k, 0:32, :], two_by_two(val_ref[k]), preferred_element_type=F32)
            half_ref[k, 0:32, :] = both[:, :128].astype(BF16)
            half_ref[k, 32:64, :] = both[:, 128:].astype(BF16)

    def cond_of(k):
        return jnp.concatenate([cond_ref[0, k], cond_ref[1, k]], axis=1)

    for k in range(N):
        pair_ref[k] = lax.dot_general(
            cond_of(k), half_ref[k], (((0,), (0,)), ((), ())), preferred_element_type=F32
        ).astype(BF16)

    for k in range(N):
        def add(n, acc):
            code = codes[k, n]
            q = code // 16
            other = code % 16
            w = w_ref[q].reshape(256, 128)
            return acc + (w * pair_ref[other]).astype(F32)

        acc = lax.fori_loop(0, counts[k], add, jnp.zeros((256, 128), F32))
        sum_ref[k] += jnp.dot(cond_of(k), acc.astype(BF16), preferred_element_type=F32)

    @pl.when(step == pl.num_programs(0) - 1)
    def _():
        for k in range(N):
            both = jnp.concatenate([sum_ref[k, 0:32, :], sum_ref[k, 32:64, :]], axis=1).astype(BF16)
            out_ref[k] = lax.dot_general(
                both, two_by_two(val_ref[k]), (((1,), (1,)), ((), ())), preferred_element_type=F32
            ).astype(BF16)


def apply(codes, counts, u, val, cond, w, name):
    grid_spec = pltpu.PrefetchScalarGridSpec(
        num_scalar_prefetch=2,
        grid=(4,),
        in_specs=[
            pl.BlockSpec(u.shape, lambda s, *_: (0, 0, 0)),
            pl.BlockSpec((N, 64, 128), lambda s, *_: (0, 0, 0)),
            pl.BlockSpec((2, N, 64, 128), lambda s, *_: (s, 0, 0, 0)),
            pl.BlockSpec((16, 2, 128, 128), lambda s, *_: (0, s, 0, 0)),
        ],
        out_specs=pl.BlockSpec((N, 32, 128), lambda s, *_: (0, 0, 0)),
        scratch_shapes=[
            pltpu.VMEM((N, 64, 128), BF16),
            pltpu.VMEM((N, 256, 128), BF16),
            pltpu.VMEM((N, 64, 128), F32),
        ],
    )
    return pl.pallas_call(
        apply_kernel,
        out_shape=jax.ShapeDtypeStruct((N, 32, 128), BF16),
        grid_spec=grid_spec,
        compiler_params=pltpu.CompilerParams(vmem_limit_bytes=VMEM_LIMIT),
        name=name,
    )(codes, counts, u, val, cond, w)


def reduce_scatter(ka, pb, part_ref, first_ref, cut_ref, second_ref, a_s, a_r, b_s, b_r):
    a_c = send_all("ka", ka, lambda p: part_ref.at[p], lambda p: first_ref.at[p], a_s, a_r)
    first_ref[ka] = part_ref[ka]
    recv_all("ka", ka, lambda p: first_ref.at[p], a_s, a_r)
    row = jnp.sum(first_ref[...].astype(F32), axis=0)
    for i in range(N):
        cut_ref[i] = row[2 * i : 2 * i + 2, :]
    b_c = send_all("pb", pb, lambda p: cut_ref.at[p], lambda p: second_ref.at[p], b_s, b_r)
    second_ref[pb] = cut_ref[pb]
    recv_all("pb", pb, lambda p: second_ref.at[p], b_s, b_r)
    return jnp.sum(second_ref[...], axis=0), a_c + b_c


def safe_divide(top, bottom):
    return jnp.where(bottom > 0, top / jnp.where(bottom > 0, bottom, 1.0), 0.0)


def middle_kernel(
    entries, factor,
    part_ref, dip_ref, energy_ref, row_ref, dips_ref,
    u_out, own_out, scalar_out,
    first_ref, cut_ref, second_ref, image_ref, mine_ref, flat_ref, msg_ref, all_ref,
    a_s, a_r, b_s, b_r, c_s, c_r, d_s, d_r,
):
    ka = lax.axis_index("ka")
    pb = lax.axis_index("pb")
    barrier_all(ka, pb)
    kernel_out, copies = reduce_scatter(
        ka, pb, part_ref, first_ref, cut_ref, second_ref, a_s, a_r, b_s, b_r
    )
    squares = read_stat(dips_ref[:, 32:48, :].astype(F32), 0)
    scale = 1.0 / jnp.sqrt(jnp.sum(squares, axis=0) / entries + EPSILON)
    own = dip_ref[...] * scale
    mine_ref[...] = energy_ref[...] * own - factor * scale * kernel_out
    image_ref[pb] = mine_ref[...]
    copies += send_all("pb", pb, lambda p: mine_ref, lambda p: image_ref.at[p], c_s, c_r)
    vector = row_ref[...] * scale
    norm = total(vector * vector)
    recv_all("pb", pb, lambda p: image_ref.at[p], c_s, c_r)
    image = image_ref[...]
    inner = total(vector * image)
    slope = safe_divide(inner, norm)
    rest = image - slope * vector
    left = total(rest * rest)
    for i in range(N):
        flat_ref[2 * i : 2 * i + 2, :] = rest[i]
    msg_ref[0:32, :] = flat_ref[...].astype(BF16)
    msg_ref[32:48, :] = stat_rows([inner, slope, left, norm])
    all_ref[ka] = msg_ref[...]
    copies += send_all("ka", ka, lambda p: msg_ref, lambda p: all_ref.at[p], d_s, d_r)
    recv_all("ka", ka, lambda p: all_ref.at[p], d_s, d_r)
    stats = all_ref[:, 32:48, :].astype(F32)
    slopes = read_stat(stats, 1)
    alpha = jnp.sum(read_stat(stats, 0), axis=0) / entries
    off = slopes - alpha
    square = jnp.sum(read_stat(stats, 2) + read_stat(stats, 3) * off * off, axis=0) / entries
    beta = jnp.sqrt(square + EPSILON)
    scaled = off * scale
    for k in range(N):
        u_out[k] = (
            all_ref[k, 0:32, :].astype(F32) + scaled[k] * dips_ref[k, 0:32, :].astype(F32)
        ).astype(BF16)
    own_out[0] = (mine_ref[...] - alpha * own) / beta
    own_out[1] = own
    scalar_out[...] = jnp.concatenate([alpha, beta], axis=0)
    for copy in copies:
        copy.wait_send()


def middle(entries, factor, part, dipole, energy, row, dips):
    sem = pltpu.SemaphoreType.DMA
    vmem = pl.BlockSpec(memory_space=pltpu.VMEM)
    return pl.pallas_call(
        functools.partial(middle_kernel, entries, factor),
        out_shape=[
            jax.ShapeDtypeStruct((N, 32, 128), BF16),
            jax.ShapeDtypeStruct((2, 2, 128), F32),
            jax.ShapeDtypeStruct((2, 128), F32),
        ],
        in_specs=[vmem] * 5,
        out_specs=[vmem] * 3,
        scratch_shapes=[
            pltpu.VMEM((N, 32, 128), BF16),
            pltpu.VMEM((N, 2, 128), F32),
            pltpu.VMEM((N, 2, 128), F32),
            pltpu.VMEM((N, 2, 128), F32),
            pltpu.VMEM((2, 128), F32),
            pltpu.VMEM((32, 128), F32),
            pltpu.VMEM((48, 128), BF16),
            pltpu.VMEM((N, 48, 128), BF16),
        ]
        + [sem((16,))] * 8,
        compiler_params=pltpu.CompilerParams(
            collective_id=1, has_side_effects=True, vmem_limit_bytes=VMEM_LIMIT
        ),
        name="middle",
    )(part, dipole, energy, row, dips)


def last_kernel(
    entries, factor,
    part_ref, energy_ref, own_ref, scalar_ref,
    u_out, coef_out,
    first_ref, cut_ref, second_ref, stat_ref, stats_ref, msg_ref, all_ref,
    a_s, a_r, b_s, b_r, c_s, c_r, d_s, d_r,
):
    ka = lax.axis_index("ka")
    pb = lax.axis_index("pb")
    barrier_all(ka, pb)
    kernel_out, copies = reduce_scatter(
        ka, pb, part_ref, first_ref, cut_ref, second_ref, a_s, a_r, b_s, b_r
    )
    alpha_zero = scalar_ref[0:1, :]
    beta_zero = scalar_ref[1:2, :]
    vector = own_ref[0]
    former = own_ref[1]
    image = energy_ref[...] * vector - factor / beta_zero * kernel_out
    rest = image - beta_zero * former
    norm = total(vector * vector)
    cross = total(vector * rest)
    slope = safe_divide(cross, norm)
    gap = rest - slope * vector
    row = lax.broadcasted_iota(jnp.int32, (8, 128), 0)

    def pack(values):
        block = jnp.zeros((8, 128), F32)
        for i, value in enumerate(values):
            block = jnp.where(row == i, jnp.broadcast_to(value, (8, 128)), block)
        return block

    stat_ref[...] = pack([total(vector * image), slope, total(gap * gap), norm])
    stats_ref[pb] = stat_ref[...]
    copies += send_all("pb", pb, lambda p: stat_ref, lambda p: stats_ref.at[p], c_s, c_r)
    recv_all("pb", pb, lambda p: stats_ref.at[p], c_s, c_r)

    def merge(block):
        inner, slopes, left, norms = [block[:, i : i + 1, :] for i in range(4)]
        norm = jnp.sum(norms, axis=0)
        slope = safe_divide(jnp.sum(norms * slopes, axis=0), norm)
        off = slopes - slope
        return jnp.sum(inner, axis=0), slope, jnp.sum(left + norms * off * off, axis=0), norm

    msg_ref[...] = pack(merge(stats_ref[...]))
    all_ref[ka] = msg_ref[...]
    copies += send_all("ka", ka, lambda p: msg_ref, lambda p: all_ref.at[p], d_s, d_r)
    recv_all("ka", ka, lambda p: all_ref.at[p], d_s, d_r)
    inner, slope, left, norm = merge(all_ref[...])
    alpha = inner / entries
    off = slope - alpha
    beta = jnp.sqrt((left + norm * off * off) / entries + EPSILON)
    u_out[...] = (rest - alpha * vector) / beta
    lane = lax.broadcasted_iota(jnp.int32, (1, 128), 1)
    coef_out[...] = jnp.where(
        lane == 0, alpha_zero, jnp.where(lane == 1, alpha, jnp.where(lane == 2, beta_zero, beta))
    )
    for copy in copies:
        copy.wait_send()


def last(entries, factor, part, energy, own, scalars):
    sem = pltpu.SemaphoreType.DMA
    vmem = pl.BlockSpec(memory_space=pltpu.VMEM)
    return pl.pallas_call(
        functools.partial(last_kernel, entries, factor),
        out_shape=[jax.ShapeDtypeStruct((2, 128), F32), jax.ShapeDtypeStruct((1, 128), F32)],
        in_specs=[vmem] * 4,
        out_specs=[vmem] * 2,
        scratch_shapes=[
            pltpu.VMEM((N, 32, 128), BF16),
            pltpu.VMEM((N, 2, 128), F32),
            pltpu.VMEM((N, 2, 128), F32),
            pltpu.VMEM((8, 128), F32),
            pltpu.VMEM((N, 8, 128), F32),
            pltpu.VMEM((8, 128), F32),
            pltpu.VMEM((N, 8, 128), F32),
        ]
        + [sem((16,))] * 8,
        compiler_params=pltpu.CompilerParams(
            collective_id=2, has_side_effects=True, vmem_limit_bytes=VMEM_LIMIT
        ),
        name="last",
    )(part, energy, own, scalars)


def per_device(dipole, energy, cond_amp, val_amp, screened, window):
    entries = 16 * 4096
    factor = 1.0 / (2048 * math.sqrt(entries))
    dipole = dipole.reshape(2, 128)
    energy = energy.reshape(2, 128)
    codes, counts = pair_lists(window)
    cond, val, w, row, dips = gather(
        dipole, cond_amp[0], val_amp[0], screened.reshape(8, 8, 2, 128, 128)
    )
    part = apply(codes, counts, dips, val, cond, w, "apply_first")
    vector, own, scalars = middle(entries, factor, part, dipole, energy, row, dips)
    part = apply(codes, counts, vector, val, cond, w, "apply_second")
    out, coef = last(entries, factor, part, energy, own, scalars)
    return coef[0, :4], out.reshape(1, 256)


def solution(mesh):
    in_specs = (
        P("ka", "pb"),
        P("ka", "pb"),
        P("ka", None, "pb"),
        P("pb", None, "ka"),
        P("pb", None, "ka"),
        P(),
    )
    out_specs = (P(), P("ka", "pb"))
    return jax.shard_map(
        per_device, mesh=mesh, in_specs=in_specs, out_specs=out_specs, check_vma=False
    )
```

```python
import functools
import math

import jax
import jax.numpy as jnp
from jax import lax
from jax.experimental import pallas as pl
from jax.experimental.pallas import tpu as pltpu
from jax.sharding import PartitionSpec as P

EPSILON = 1e-06
F32 = jnp.float32
BF16 = jnp.bfloat16
N = 16
NT = (((1,), (1,)), ((), ()))
MESH = pl.DeviceIdType.MESH


def ring_peers(me):
    return [lax.rem(me + o, N) for o in range(1, N)]


def signal_all(barrier, ka, pb):
    for peer in ring_peers(ka):
        pl.semaphore_signal(barrier, inc=1, device_id={"ka": peer}, device_id_type=MESH)
    for peer in ring_peers(pb):
        pl.semaphore_signal(barrier, inc=1, device_id={"pb": peer}, device_id_type=MESH)


def send_one(source, target, send_sem, recv_sem, device):
    copy = pltpu.make_async_remote_copy(
        src_ref=source,
        dst_ref=target,
        send_sem=send_sem,
        recv_sem=recv_sem,
        device_id=device,
        device_id_type=MESH,
    )
    copy.start()
    return copy


def recv_one(target, send_sem, recv_sem, device):
    pltpu.make_async_remote_copy(
        src_ref=target,
        dst_ref=target,
        send_sem=send_sem,
        recv_sem=recv_sem,
        device_id=device,
        device_id_type=MESH,
    ).wait_recv()


def send_all(axis, me, source, target, sems):
    return [
        send_one(source(peer), target(me), sems[0].at[o], sems[1].at[me], {axis: peer})
        for o, peer in enumerate(ring_peers(me))
    ]


def recv_all(axis, me, target, sems):
    for o, peer in enumerate(ring_peers(me)):
        recv_one(target(peer), sems[0].at[o], sems[1].at[peer], {axis: peer})


def total(x):
    while x.ndim > 2:
        x = jnp.sum(x, axis=0)
    return jnp.sum(jnp.sum(x, axis=0, keepdims=True), axis=1, keepdims=True)


def stat_rows(values):
    row = lax.broadcasted_iota(jnp.int32, (16, 128), 0)
    block = jnp.zeros((16, 128), F32)
    for i, value in enumerate(values):
        rest = jnp.broadcast_to(value, (16, 128))
        for part in range(3):
            piece = rest.astype(BF16).astype(F32)
            block = jnp.where(row == 3 * i + part, piece, block)
            rest = rest - piece
    return block.astype(BF16)


def read_stat(block, i):
    return block[:, 3 * i : 3 * i + 1] + block[:, 3 * i + 1 : 3 * i + 2] + block[:, 3 * i + 2 : 3 * i + 3]


def pack(values):
    row = lax.broadcasted_iota(jnp.int32, (8, 128), 0)
    block = jnp.zeros((8, 128), F32)
    for i, value in enumerate(values):
        block = jnp.where(row == i, jnp.broadcast_to(value, (8, 128)), block)
    return block


def safe_divide(top, bottom):
    return jnp.where(bottom > 0, top / jnp.where(bottom > 0, bottom, 1.0), 0.0)


def loop(count, body):
    def step(i, carry):
        body(i)
        return carry

    lax.fori_loop(0, count, step, 0)


def haydock_kernel(
    entries, factor,
    window_ref, dip_ref, energy_ref, cond_ref, val_ref, w_ref,
    u_out, coef_out,
    index_ref, perm_ref, cond_all, val_all, vv_ref, stage_ref, wt_ref,
    pack_ref, rows_ref, drow_ref, erow_ref, msg_ref, dips_ref, u_ref,
    half_ref, pair_ref, screen_ref, sum_ref, part_ref, first_ref, mine_ref, second_ref,
    after_ref, rests_ref, stat_ref, stats_ref, cut_ref,
    row_s, row_r, cond_s, cond_r, val_s, val_r, dip_s, dip_r, hop_s, hop_r, w_sem, own_sem,
    a_s, a_r, b_s, b_r, d_s, d_r, e_s, e_r,
):
    ka = lax.axis_index("ka")
    pb = lax.axis_index("pb")
    core = lax.rem(pb, 2)
    chip = pb // 2
    x = lax.rem(chip, 4)
    y = chip // 4
    across = (1 - y) * 4 + x
    barrier = pltpu.get_barrier_semaphore()
    signal_all(barrier, ka, pb)

    own_w = pltpu.make_async_copy(w_ref.at[:, :, core], stage_ref.at[pl.ds(core * 8, 8)], own_sem.at[0])
    own_w.start()
    to = lax.broadcasted_iota(jnp.int32, (64, 64), 0)
    fro = lax.broadcasted_iota(jnp.int32, (64, 64), 1)
    pick = (fro == 2 * lax.rem(to, 32) + to // 32).astype(F32).astype(BF16)
    perm_ref[...] = jnp.dot(pick, cond_ref[...], preferred_element_type=F32).astype(BF16)
    cond_all[chip, ka] = perm_ref[...]
    val_all[pb] = val_ref[...]
    pack_ref[0:2, :] = dip_ref[...]
    pack_ref[2:4, :] = energy_ref[...]
    rows_ref[pb] = pack_ref[...]
    pl.semaphore_wait(barrier, 2 * (N - 1))

    copies = send_all("ka", ka, lambda p: perm_ref, lambda p: cond_all.at[chip, p], (cond_s, cond_r))
    copies += send_all("pb", pb, lambda p: pack_ref, lambda p: rows_ref.at[p], (row_s, row_r))
    sibling = {"pb": pb + 1 - 2 * core}
    w_send = send_one(
        w_ref.at[:, :, 1 - core], stage_ref.at[pl.ds(core * 8, 8)], w_sem.at[0], w_sem.at[1], sibling
    )
    copies += [w_send]
    copies += send_all("pb", pb, lambda p: val_ref, lambda p: val_all.at[p], (val_s, val_r))

    def table(k):
        mine = window_ref[k]
        for other in range(N):
            theirs = window_ref[other]
            shift_one = jnp.bitwise_and(lax.shift_right_logical(mine, 5) - lax.shift_right_logical(theirs, 5), 3)
            shift_two = jnp.bitwise_and(lax.shift_right_logical(mine, 2) - lax.shift_right_logical(theirs, 2), 7)
            shift_three = jnp.bitwise_and(mine - theirs, 3)
            q = (shift_one * 8 + shift_two) * 4 + shift_three
            index_ref[k * N + other] = jnp.where(
                lax.shift_right_logical(q, 4) == chip, jnp.bitwise_and(q, 15), 16
            )

    loop(N, table)

    recv_all("pb", pb, lambda p: rows_ref.at[p], (row_s, row_r))
    for i in range(N):
        drow_ref[2 * i : 2 * i + 2, :] = rows_ref[i, 0:2, :]
        erow_ref[2 * i : 2 * i + 2, :] = rows_ref[i, 2:4, :]
    drow = drow_ref[...]
    msg_ref[0, 0:32, :] = drow.astype(BF16)
    msg_ref[0, 32:48, :] = stat_rows([total(drow * drow)])
    dips_ref[ka] = msg_ref[0]
    copies += send_all("ka", ka, lambda p: msg_ref.at[0], lambda p: dips_ref.at[p], (dip_s, dip_r))

    recv_all("ka", ka, lambda p: cond_all.at[chip, p], (cond_s, cond_r))
    lower = pl.ds(0, 8)
    upper = pl.ds(8, 8)
    x_chips = [y * 4 + lax.rem(x + o, 4) for o in range(1, 4)]

    def at(which):
        return {"pb": which * 2 + core}

    copies += [send_one(cond_all.at[chip], cond_all.at[chip], hop_s.at[0], hop_r.at[0], at(across))]
    for o in range(3):
        copies += [
            send_one(cond_all.at[chip], cond_all.at[chip], hop_s.at[1 + o], hop_r.at[1 + o], at(x_chips[o]))
        ]

    def turn(q):
        for j in range(8):
            wt_ref[j % 4, q, :, j // 4 * 128 : j // 4 * 128 + 128] = stage_ref[q, j].T

    own_w.wait()
    loop(8, lambda q: turn(core * 8 + q))
    for i in range(4):
        wt_ref[i, 16] = jnp.zeros((128, 256), BF16)
    recv_one(stage_ref.at[pl.ds((1 - core) * 8, 8)], w_sem.at[0], w_sem.at[1], sibling)
    loop(8, lambda q: turn((1 - core) * 8 + q))

    recv_all("pb", pb, lambda p: val_all.at[p], (val_s, val_r))

    def spread(k):
        turned = val_all[k].T
        zero = jnp.zeros_like(turned)
        vv_ref[k] = jnp.concatenate(
            [jnp.concatenate([turned, zero], axis=1), jnp.concatenate([zero, turned], axis=1)], axis=0
        )

    loop(N, spread)
    recv_all("ka", ka, lambda p: dips_ref.at[p], (dip_s, dip_r))

    def start_apply(vector_ref):
        def first(k):
            both = lax.dot_general(vv_ref[k], vector_ref[k, 0:32, :], NT, preferred_element_type=F32)
            half_ref[k, :, 0:32] = both[0:128].astype(BF16)
            half_ref[k, :, 32:64] = both[128:256].astype(BF16)
            sum_ref[k] = jnp.zeros((64, 128), F32)

        loop(N, first)

    def columns(part, k):
        return jnp.concatenate([cond_all[part, k], cond_all[part + 4, k]], axis=1)

    def apply_part(part):
        def pairs(k):
            pair_ref[k] = jnp.dot(half_ref[k], columns(part, k), preferred_element_type=F32).astype(BF16)

        def screen(k):
            for top in (0, 64):
                rows = slice(top, top + 64)
                acc = jnp.zeros((64, 256), F32)
                for other in range(0, N, 2):
                    one = wt_ref[part, index_ref[k * N + other], rows, :] * pair_ref[other, rows, :]
                    two = wt_ref[part, index_ref[k * N + other + 1], rows, :] * pair_ref[other + 1, rows, :]
                    acc = acc + (one + two).astype(F32)
                screen_ref[rows, :] = acc.astype(BF16)
            sum_ref[k] += lax.dot_general(columns(part, k), screen_ref[...], NT, preferred_element_type=F32)

        loop(N, pairs)
        loop(N, screen)

    def finish_apply(which):
        def one(k):
            both = jnp.concatenate([sum_ref[k, 0:32, :], sum_ref[k, 32:64, :]], axis=1)
            high = both.astype(BF16)
            low = (both - high.astype(F32)).astype(BF16)
            part_ref[which, k] = (
                jnp.dot(high, vv_ref[k], preferred_element_type=F32)
                + jnp.dot(low, vv_ref[k], preferred_element_type=F32)
            ).astype(BF16)

        loop(N, one)

    start_apply(dips_ref)
    recv_one(cond_all.at[across], hop_s.at[0], hop_r.at[0], at(across))
    for o in range(3):
        copies.append(
            send_one(
                cond_all.at[across, lower], cond_all.at[across, lower], hop_s.at[4 + o], hop_r.at[4 + o], at(x_chips[o])
            )
        )
    apply_part(x)
    for o in (0, 2, 1):
        back = x_chips[2 - o]
        recv_one(cond_all.at[back], hop_s.at[1 + o], hop_r.at[1 + o], at(back))
        copies.append(
            send_one(
                cond_all.at[back, upper], cond_all.at[back, upper], hop_s.at[7 + o], hop_r.at[7 + o], at(across)
            )
        )
    for o in (0, 2, 1):
        back = x_chips[2 - o]
        far = (1 - y) * 4 + lax.rem(back, 4)
        recv_one(cond_all.at[far, lower], hop_s.at[4 + o], hop_r.at[4 + o], at(back))
        recv_one(cond_all.at[far, upper], hop_s.at[7 + o], hop_r.at[7 + o], at(across))
        apply_part(lax.rem(back, 4))
    finish_apply(0)

    def reduce_rows(which):
        new = send_all(
            "ka", ka, lambda p: part_ref.at[which, p], lambda p: first_ref.at[which, p], (a_s.at[which], a_r.at[which])
        )
        first_ref[which, ka] = part_ref[which, ka]
        recv_all("ka", ka, lambda p: first_ref.at[which, p], (a_s.at[which], a_r.at[which]))
        mine_ref[which] = jnp.sum(first_ref[which].astype(F32), axis=0).astype(BF16)
        second_ref[which, pb] = mine_ref[which]
        new += send_all(
            "pb", pb, lambda p: mine_ref.at[which], lambda p: second_ref.at[which, p], (b_s.at[which], b_r.at[which])
        )
        recv_all("pb", pb, lambda p: second_ref.at[which, p], (b_s.at[which], b_r.at[which]))
        return jnp.sum(second_ref[which].astype(F32), axis=0), new

    kernel_row, new = reduce_rows(0)
    copies += new
    squares = read_stat(dips_ref[:, 32:48, :].astype(F32), 0)
    scale = 1.0 / jnp.sqrt(jnp.sum(squares, axis=0) / entries + EPSILON)
    vector = drow_ref[...] * scale
    image = erow_ref[...] * vector - factor * scale * kernel_row
    norm = total(vector * vector)
    inner = total(vector * image)
    slope = safe_divide(inner, norm)
    rest = image - slope * vector
    msg_ref[1, 0:32, :] = rest.astype(BF16)
    msg_ref[1, 32:48, :] = stat_rows([inner, slope, total(rest * rest), norm])
    rests_ref[ka] = msg_ref[1]
    copies += send_all("ka", ka, lambda p: msg_ref.at[1], lambda p: rests_ref.at[p], (d_s, d_r))
    recv_all("ka", ka, lambda p: rests_ref.at[p], (d_s, d_r))
    stats = rests_ref[:, 32:48, :].astype(F32)
    alpha_zero = jnp.sum(read_stat(stats, 0), axis=0) / entries
    off = read_stat(stats, 1) - alpha_zero
    square = jnp.sum(read_stat(stats, 2) + read_stat(stats, 3) * off * off, axis=0) / entries
    beta_zero = jnp.sqrt(square + EPSILON)
    scaled = off * scale
    for k in range(N):
        u_ref[k] = (
            rests_ref[k, 0:32, :].astype(F32) + scaled[k] * dips_ref[k, 0:32, :].astype(F32)
        ).astype(BF16)
    after_ref[0] = vector
    after_ref[1] = (image - alpha_zero * vector) / beta_zero

    start_apply(u_ref)
    loop(4, apply_part)
    finish_apply(1)
    kernel_row, new = reduce_rows(1)
    copies += new
    former = after_ref[0]
    vector = after_ref[1]
    image = erow_ref[...] * vector - factor / beta_zero * kernel_row
    rest = image - beta_zero * former
    norm = total(vector * vector)
    slope = safe_divide(total(vector * rest), norm)
    gap = rest - slope * vector
    stat_ref[...] = pack([total(vector * image), slope, total(gap * gap), norm])
    stats_ref[ka] = stat_ref[...]
    copies += send_all("ka", ka, lambda p: stat_ref, lambda p: stats_ref.at[p], (e_s, e_r))
    recv_all("ka", ka, lambda p: stats_ref.at[p], (e_s, e_r))
    inners, slopes, lefts, norms = [stats_ref[:, i : i + 1, :] for i in range(4)]
    alpha = jnp.sum(inners, axis=0) / entries
    off = slopes - alpha
    beta = jnp.sqrt(jnp.sum(lefts + norms * off * off, axis=0) / entries + EPSILON)
    last = (rest - alpha * vector) / beta
    for i in range(N):
        cut_ref[i] = last[2 * i : 2 * i + 2, :]
    u_out[...] = cut_ref[pb]
    lane = lax.broadcasted_iota(jnp.int32, (1, 128), 1)
    coef_out[...] = jnp.where(
        lane == 0, alpha_zero, jnp.where(lane == 1, alpha, jnp.where(lane == 2, beta_zero, beta))
    )
    for copy in copies:
        copy.wait_send()


def haydock(entries, factor, *args):
    sem = pltpu.SemaphoreType.DMA
    vmem = pl.BlockSpec(memory_space=pltpu.VMEM)
    pair = [sem((N,)), sem((N,))]
    return pl.pallas_call(
        functools.partial(haydock_kernel, entries, factor),
        out_shape=[jax.ShapeDtypeStruct((2, 128), F32), jax.ShapeDtypeStruct((1, 128), F32)],
        in_specs=[pl.BlockSpec(memory_space=pltpu.SMEM)] + [vmem] * 4 + [pl.BlockSpec(memory_space=pl.ANY)],
        out_specs=[vmem] * 2,
        scratch_shapes=[
            pltpu.SMEM((N * N,), jnp.int32),
            pltpu.VMEM((64, 128), BF16),
            pltpu.VMEM((8, N, 64, 128), BF16),
            pltpu.VMEM((N, 64, 128), BF16),
            pltpu.VMEM((N, 256, 128), BF16),
            pltpu.VMEM((16, 8, 128, 128), BF16),
            pltpu.VMEM((4, 17, 128, 256), BF16),
            pltpu.VMEM((4, 128), F32),
            pltpu.VMEM((N, 4, 128), F32),
            pltpu.VMEM((32, 128), F32),
            pltpu.VMEM((32, 128), F32),
            pltpu.VMEM((2, 48, 128), BF16),
            pltpu.VMEM((N, 48, 128), BF16),
            pltpu.VMEM((N, 32, 128), BF16),
            pltpu.VMEM((N, 128, 64), BF16),
            pltpu.VMEM((N, 128, 256), BF16),
            pltpu.VMEM((128, 256), BF16),
            pltpu.VMEM((N, 64, 128), F32),
            pltpu.VMEM((2, N, 32, 128), BF16),
            pltpu.VMEM((2, N, 32, 128), BF16),
            pltpu.VMEM((2, 32, 128), BF16),
            pltpu.VMEM((2, N, 32, 128), BF16),
            pltpu.VMEM((2, 32, 128), F32),
            pltpu.VMEM((N, 48, 128), BF16),
            pltpu.VMEM((8, 128), F32),
            pltpu.VMEM((N, 8, 128), F32),
            pltpu.VMEM((N, 2, 128), F32),
        ]
        + pair * 5
        + [sem((2,)), sem((1,))]
        + [sem((2, N))] * 4
        + pair * 2,
        compiler_params=pltpu.CompilerParams(
            collective_id=0, has_side_effects=True, vmem_limit_bytes=48 * 1024 * 1024
        ),
        name="haydock",
    )(*args)


def per_device(dipole, energy, cond_amp, val_amp, screened, window):
    entries = 16 * 4096
    factor = 1.0 / (2048 * math.sqrt(entries))
    out, coef = haydock(
        entries,
        factor,
        window,
        dipole.reshape(2, 128),
        energy.reshape(2, 128),
        cond_amp[0],
        val_amp[0],
        screened.reshape(8, 8, 2, 128, 128),
    )
    return coef[0, :4], out.reshape(1, 256)


def solution(mesh):
    in_specs = (
        P("ka", "pb"),
        P("ka", "pb"),
        P("ka", None, "pb"),
        P("pb", None, "ka"),
        P("pb", None, "ka"),
        P(),
    )
    out_specs = (P(), P("ka", "pb"))
    return jax.shard_map(
        per_device, mesh=mesh, in_specs=in_specs, out_specs=out_specs, check_vma=False
    )
```

```python
import functools
import math

import jax
import jax.numpy as jnp
from jax import lax
from jax.experimental import pallas as pl
from jax.experimental.pallas import tpu as pltpu
from jax.sharding import PartitionSpec as P

EPSILON = 1e-06
F32 = jnp.float32
BF16 = jnp.bfloat16
N = 16
NT = (((1,), (1,)), ((), ()))
MESH = pl.DeviceIdType.MESH


def ring_peers(me):
    return [lax.rem(me + o, N) for o in range(1, N)]


def signal_all(barrier, ka, pb):
    for peer in ring_peers(ka):
        pl.semaphore_signal(barrier, inc=1, device_id={"ka": peer}, device_id_type=MESH)
    for peer in ring_peers(pb):
        pl.semaphore_signal(barrier, inc=1, device_id={"pb": peer}, device_id_type=MESH)


def send_one(source, target, send_sem, recv_sem, device):
    copy = pltpu.make_async_remote_copy(
        src_ref=source,
        dst_ref=target,
        send_sem=send_sem,
        recv_sem=recv_sem,
        device_id=device,
        device_id_type=MESH,
    )
    copy.start()
    return copy


def recv_one(target, send_sem, recv_sem, device):
    pltpu.make_async_remote_copy(
        src_ref=target,
        dst_ref=target,
        send_sem=send_sem,
        recv_sem=recv_sem,
        device_id=device,
        device_id_type=MESH,
    ).wait_recv()


def send_all(axis, me, source, target, sems):
    return [
        send_one(source(peer), target(me), sems[0].at[o], sems[1].at[me], {axis: peer})
        for o, peer in enumerate(ring_peers(me))
    ]


def recv_all(axis, me, target, sems):
    for o, peer in enumerate(ring_peers(me)):
        recv_one(target(peer), sems[0].at[o], sems[1].at[peer], {axis: peer})


def total(x):
    while x.ndim > 2:
        x = jnp.sum(x, axis=0)
    return jnp.sum(jnp.sum(x, axis=0, keepdims=True), axis=1, keepdims=True)


def stat_rows(values):
    row = lax.broadcasted_iota(jnp.int32, (16, 128), 0)
    block = jnp.zeros((16, 128), F32)
    for i, value in enumerate(values):
        rest = jnp.broadcast_to(value, (16, 128))
        for part in range(3):
            piece = rest.astype(BF16).astype(F32)
            block = jnp.where(row == 3 * i + part, piece, block)
            rest = rest - piece
    return block.astype(BF16)


def read_stat(block, i):
    return block[:, 3 * i : 3 * i + 1] + block[:, 3 * i + 1 : 3 * i + 2] + block[:, 3 * i + 2 : 3 * i + 3]


def pack(values):
    row = lax.broadcasted_iota(jnp.int32, (8, 128), 0)
    block = jnp.zeros((8, 128), F32)
    for i, value in enumerate(values):
        block = jnp.where(row == i, jnp.broadcast_to(value, (8, 128)), block)
    return block


def safe_divide(top, bottom):
    return jnp.where(bottom > 0, top / jnp.where(bottom > 0, bottom, 1.0), 0.0)


def loop(count, body):
    def step(i, carry):
        body(i)
        return carry

    lax.fori_loop(0, count, step, 0)


def haydock_kernel(
    entries, factor,
    window_ref, dip_ref, energy_ref, cond_ref, val_ref, w_ref,
    u_out, coef_out,
    grid_ref, index_ref, perm_ref, cond_all, val_all, vv_ref, stage_ref, wt_ref,
    pack_ref, rows_ref, drow_ref, erow_ref, msg_ref, dips_ref, u_ref,
    half_ref, pair_ref, screen_ref, sum_ref, part_ref, first_ref, mine_ref, second_ref,
    after_ref, rests_ref, stat_ref, stats_ref, cut_ref,
    row_s, row_r, cond_s, cond_r, val_s, val_r, dip_s, dip_r, hop_s, hop_r, w_sem, own_sem,
    a_s, a_r, b_s, b_r, d_s, d_r, e_s, e_r,
):
    ka = lax.axis_index("ka")
    pb = lax.axis_index("pb")
    core = lax.rem(pb, 2)
    chip = pb // 2
    x = lax.rem(chip, 4)
    y = chip // 4
    across = (1 - y) * 4 + x
    barrier = pltpu.get_barrier_semaphore()
    signal_all(barrier, ka, pb)

    loads = [
        pltpu.make_async_copy(source, target, own_sem.at[1 + i])
        for i, (source, target) in enumerate(
            [
                (cond_ref, perm_ref.at[0]),
                (dip_ref, pack_ref.at[0]),
                (energy_ref, pack_ref.at[1]),
                (val_ref, val_all.at[pb]),
                (window_ref, grid_ref),
            ]
        )
    ]
    for load in loads:
        load.start()
    own_w = pltpu.make_async_copy(w_ref.at[:, :, core], stage_ref.at[pl.ds(core * 8, 8)], own_sem.at[0])
    own_w.start()
    to = lax.broadcasted_iota(jnp.int32, (64, 64), 0)
    fro = lax.broadcasted_iota(jnp.int32, (64, 64), 1)
    pick = (fro == 2 * lax.rem(to, 32) + to // 32).astype(F32).astype(BF16)
    for load in loads:
        load.wait()
    perm_ref[1] = jnp.dot(pick, perm_ref[0], preferred_element_type=F32).astype(BF16)
    cond_all[chip, ka] = perm_ref[1]
    rows_ref[pb] = pack_ref[...]
    pl.semaphore_wait(barrier, 2 * (N - 1))

    copies = send_all("ka", ka, lambda p: perm_ref.at[1], lambda p: cond_all.at[chip, p], (cond_s, cond_r))
    copies += send_all("pb", pb, lambda p: pack_ref, lambda p: rows_ref.at[p], (row_s, row_r))
    sibling = {"pb": pb + 1 - 2 * core}
    w_send = send_one(
        w_ref.at[:, :, 1 - core], stage_ref.at[pl.ds(core * 8, 8)], w_sem.at[0], w_sem.at[1], sibling
    )
    copies += [w_send]
    copies += send_all("pb", pb, lambda p: val_all.at[pb], lambda p: val_all.at[p], (val_s, val_r))

    def table(k):
        mine = grid_ref[k]
        for other in range(N):
            theirs = grid_ref[other]
            shift_one = jnp.bitwise_and(lax.shift_right_logical(mine, 5) - lax.shift_right_logical(theirs, 5), 3)
            shift_two = jnp.bitwise_and(lax.shift_right_logical(mine, 2) - lax.shift_right_logical(theirs, 2), 7)
            shift_three = jnp.bitwise_and(mine - theirs, 3)
            q = (shift_one * 8 + shift_two) * 4 + shift_three
            index_ref[k * N + other] = jnp.where(
                lax.shift_right_logical(q, 4) == chip, jnp.bitwise_and(q, 15), 16
            )

    loop(N, table)

    recv_all("pb", pb, lambda p: rows_ref.at[p], (row_s, row_r))
    for i in range(N):
        drow_ref[2 * i : 2 * i + 2, :] = rows_ref[i, 0]
        erow_ref[2 * i : 2 * i + 2, :] = rows_ref[i, 1]
    drow = drow_ref[...]
    msg_ref[0, 0:32, :] = drow.astype(BF16)
    msg_ref[0, 32:48, :] = stat_rows([total(drow * drow)])
    dips_ref[ka] = msg_ref[0]
    copies += send_all("ka", ka, lambda p: msg_ref.at[0], lambda p: dips_ref.at[p], (dip_s, dip_r))

    recv_all("ka", ka, lambda p: cond_all.at[chip, p], (cond_s, cond_r))
    lower = pl.ds(0, 8)
    upper = pl.ds(8, 8)
    x_chips = [y * 4 + lax.rem(x + o, 4) for o in range(1, 4)]

    def at(which):
        return {"pb": which * 2 + core}

    copies += [send_one(cond_all.at[chip], cond_all.at[chip], hop_s.at[0], hop_r.at[0], at(across))]
    for o in range(3):
        copies += [
            send_one(cond_all.at[chip], cond_all.at[chip], hop_s.at[1 + o], hop_r.at[1 + o], at(x_chips[o]))
        ]

    def turn(q):
        for j in range(8):
            wt_ref[j % 4, q, :, j // 4 * 128 : j // 4 * 128 + 128] = stage_ref[q, j].T

    own_w.wait()
    loop(8, lambda q: turn(core * 8 + q))
    for i in range(4):
        wt_ref[i, 16] = jnp.zeros((128, 256), BF16)
    recv_one(stage_ref.at[pl.ds((1 - core) * 8, 8)], w_sem.at[0], w_sem.at[1], sibling)
    loop(8, lambda q: turn((1 - core) * 8 + q))

    recv_all("pb", pb, lambda p: val_all.at[p], (val_s, val_r))

    def spread(k):
        turned = val_all[k].T
        zero = jnp.zeros_like(turned)
        vv_ref[k] = jnp.concatenate(
            [jnp.concatenate([turned, zero], axis=1), jnp.concatenate([zero, turned], axis=1)], axis=0
        )

    loop(N, spread)
    recv_all("ka", ka, lambda p: dips_ref.at[p], (dip_s, dip_r))

    def start_apply(vector_ref):
        for k in range(N):
            both = lax.dot_general(vv_ref[k], vector_ref[k, 0:32, :], NT, preferred_element_type=F32)
            half_ref[k, :, 0:32] = both[0:128].astype(BF16)
            half_ref[k, :, 32:64] = both[128:256].astype(BF16)
            sum_ref[k] = jnp.zeros((64, 128), F32)

    def columns(part, k):
        return jnp.concatenate([cond_all[part, k], cond_all[part + 4, k]], axis=1)

    def apply_part(part):
        def screen(k):
            acc = jnp.zeros((128, 256), BF16)
            for other in range(N):
                acc = acc + wt_ref[part, index_ref[k * N + other]] * pair_ref[other]
            screen_ref[k] = acc

        for k in range(N):
            pair_ref[k] = jnp.dot(half_ref[k], columns(part, k), preferred_element_type=F32).astype(BF16)
        loop(N, screen)
        for k in range(N):
            sum_ref[k] += lax.dot_general(columns(part, k), screen_ref[k], NT, preferred_element_type=F32)

    def finish_apply(which):
        for k in range(N):
            both = jnp.concatenate([sum_ref[k, 0:32, :], sum_ref[k, 32:64, :]], axis=1)
            high = both.astype(BF16)
            low = (both - high.astype(F32)).astype(BF16)
            part_ref[which, k] = (
                jnp.dot(high, vv_ref[k], preferred_element_type=F32)
                + jnp.dot(low, vv_ref[k], preferred_element_type=F32)
            ).astype(BF16)

    start_apply(dips_ref)
    recv_one(cond_all.at[across], hop_s.at[0], hop_r.at[0], at(across))
    for o in range(3):
        copies.append(
            send_one(
                cond_all.at[across, lower], cond_all.at[across, lower], hop_s.at[4 + o], hop_r.at[4 + o], at(x_chips[o])
            )
        )
    apply_part(x)
    for o in (0, 2, 1):
        back = x_chips[2 - o]
        recv_one(cond_all.at[back], hop_s.at[1 + o], hop_r.at[1 + o], at(back))
        copies.append(
            send_one(
                cond_all.at[back, upper], cond_all.at[back, upper], hop_s.at[7 + o], hop_r.at[7 + o], at(across)
            )
        )
    for o in (0, 2, 1):
        back = x_chips[2 - o]
        far = (1 - y) * 4 + lax.rem(back, 4)
        recv_one(cond_all.at[far, lower], hop_s.at[4 + o], hop_r.at[4 + o], at(back))
        recv_one(cond_all.at[far, upper], hop_s.at[7 + o], hop_r.at[7 + o], at(across))
        apply_part(lax.rem(back, 4))
    finish_apply(0)

    def reduce_rows(which):
        new = send_all(
            "ka", ka, lambda p: part_ref.at[which, p], lambda p: first_ref.at[which, p], (a_s.at[which], a_r.at[which])
        )
        first_ref[which, ka] = part_ref[which, ka]
        recv_all("ka", ka, lambda p: first_ref.at[which, p], (a_s.at[which], a_r.at[which]))
        mine_ref[which] = jnp.sum(first_ref[which].astype(F32), axis=0).astype(BF16)
        second_ref[which, pb] = mine_ref[which]
        new += send_all(
            "pb", pb, lambda p: mine_ref.at[which], lambda p: second_ref.at[which, p], (b_s.at[which], b_r.at[which])
        )
        recv_all("pb", pb, lambda p: second_ref.at[which, p], (b_s.at[which], b_r.at[which]))
        return jnp.sum(second_ref[which].astype(F32), axis=0), new

    kernel_row, new = reduce_rows(0)
    copies += new
    squares = read_stat(dips_ref[:, 32:48, :].astype(F32), 0)
    scale = 1.0 / jnp.sqrt(jnp.sum(squares, axis=0) / entries + EPSILON)
    vector = drow_ref[...] * scale
    image = erow_ref[...] * vector - factor * scale * kernel_row
    norm = total(vector * vector)
    inner = total(vector * image)
    slope = safe_divide(inner, norm)
    rest = image - slope * vector
    msg_ref[1, 0:32, :] = rest.astype(BF16)
    msg_ref[1, 32:48, :] = stat_rows([inner, slope, total(rest * rest), norm])
    rests_ref[ka] = msg_ref[1]
    copies += send_all("ka", ka, lambda p: msg_ref.at[1], lambda p: rests_ref.at[p], (d_s, d_r))
    recv_all("ka", ka, lambda p: rests_ref.at[p], (d_s, d_r))
    stats = rests_ref[:, 32:48, :].astype(F32)
    alpha_zero = jnp.sum(read_stat(stats, 0), axis=0) / entries
    off = read_stat(stats, 1) - alpha_zero
    square = jnp.sum(read_stat(stats, 2) + read_stat(stats, 3) * off * off, axis=0) / entries
    beta_zero = jnp.sqrt(square + EPSILON)
    scaled = off * scale
    for k in range(N):
        u_ref[k] = (
            rests_ref[k, 0:32, :].astype(F32) + scaled[k] * dips_ref[k, 0:32, :].astype(F32)
        ).astype(BF16)
    after_ref[0] = vector
    after_ref[1] = (image - alpha_zero * vector) / beta_zero

    start_apply(u_ref)
    loop(4, apply_part)
    finish_apply(1)
    kernel_row, new = reduce_rows(1)
    copies += new
    former = after_ref[0]
    vector = after_ref[1]
    image = erow_ref[...] * vector - factor / beta_zero * kernel_row
    rest = image - beta_zero * former
    norm = total(vector * vector)
    slope = safe_divide(total(vector * rest), norm)
    gap = rest - slope * vector
    stat_ref[...] = pack([total(vector * image), slope, total(gap * gap), norm])
    stats_ref[ka] = stat_ref[...]
    copies += send_all("ka", ka, lambda p: stat_ref, lambda p: stats_ref.at[p], (e_s, e_r))
    recv_all("ka", ka, lambda p: stats_ref.at[p], (e_s, e_r))
    inners, slopes, lefts, norms = [stats_ref[:, i : i + 1, :] for i in range(4)]
    alpha = jnp.sum(inners, axis=0) / entries
    off = slopes - alpha
    beta = jnp.sqrt(jnp.sum(lefts + norms * off * off, axis=0) / entries + EPSILON)
    last = (rest - alpha * vector) / beta
    for i in range(N):
        cut_ref[i] = last[2 * i : 2 * i + 2, :]
    u_out[...] = cut_ref[pb]
    lane = lax.broadcasted_iota(jnp.int32, (1, 128), 1)
    coef_out[...] = jnp.where(
        lane == 0, alpha_zero, jnp.where(lane == 1, alpha, jnp.where(lane == 2, beta_zero, beta))
    )
    for copy in copies:
        copy.wait_send()


def haydock(entries, factor, *args):
    sem = pltpu.SemaphoreType.DMA
    vmem = pl.BlockSpec(memory_space=pltpu.VMEM)
    pair = [sem((N,)), sem((N,))]
    return pl.pallas_call(
        functools.partial(haydock_kernel, entries, factor),
        out_shape=[jax.ShapeDtypeStruct((2, 128), F32), jax.ShapeDtypeStruct((1, 128), F32)],
        in_specs=[pl.BlockSpec(memory_space=pl.ANY)] * 6,
        out_specs=[vmem] * 2,
        scratch_shapes=[
            pltpu.SMEM((N,), jnp.int32),
            pltpu.SMEM((N * N,), jnp.int32),
            pltpu.VMEM((2, 64, 128), BF16),
            pltpu.VMEM((8, N, 64, 128), BF16),
            pltpu.VMEM((N, 64, 128), BF16),
            pltpu.VMEM((N, 256, 128), BF16),
            pltpu.VMEM((16, 8, 128, 128), BF16),
            pltpu.VMEM((4, 17, 128, 256), BF16),
            pltpu.VMEM((2, 2, 128), F32),
            pltpu.VMEM((N, 2, 2, 128), F32),
            pltpu.VMEM((32, 128), F32),
            pltpu.VMEM((32, 128), F32),
            pltpu.VMEM((2, 48, 128), BF16),
            pltpu.VMEM((N, 48, 128), BF16),
            pltpu.VMEM((N, 32, 128), BF16),
            pltpu.VMEM((N, 128, 64), BF16),
            pltpu.VMEM((N, 128, 256), BF16),
            pltpu.VMEM((N, 128, 256), BF16),
            pltpu.VMEM((N, 64, 128), F32),
            pltpu.VMEM((2, N, 32, 128), BF16),
            pltpu.VMEM((2, N, 32, 128), BF16),
            pltpu.VMEM((2, 32, 128), BF16),
            pltpu.VMEM((2, N, 32, 128), BF16),
            pltpu.VMEM((2, 32, 128), F32),
            pltpu.VMEM((N, 48, 128), BF16),
            pltpu.VMEM((8, 128), F32),
            pltpu.VMEM((N, 8, 128), F32),
            pltpu.VMEM((N, 2, 128), F32),
        ]
        + pair * 5
        + [sem((2,)), sem((6,))]
        + [sem((2, N))] * 4
        + pair * 2,
        compiler_params=pltpu.CompilerParams(
            collective_id=0, has_side_effects=True, vmem_limit_bytes=48 * 1024 * 1024
        ),
        name="haydock",
    )(*args)


def per_device(dipole, energy, cond_amp, val_amp, screened, window):
    entries = 16 * 4096
    factor = 1.0 / (2048 * math.sqrt(entries))
    out, coef = haydock(
        entries,
        factor,
        window,
        dipole.reshape(2, 128),
        energy.reshape(2, 128),
        cond_amp[0],
        val_amp[0],
        screened.reshape(8, 8, 2, 128, 128),
    )
    return coef[0, :4], out.reshape(1, 256)


def solution(mesh):
    in_specs = (
        P("ka", "pb"),
        P("ka", "pb"),
        P("ka", None, "pb"),
        P("pb", None, "ka"),
        P("pb", None, "ka"),
        P(),
    )
    out_specs = (P(), P("ka", "pb"))
    return jax.shard_map(
        per_device, mesh=mesh, in_specs=in_specs, out_specs=out_specs, check_vma=False
    )
```

```python
import functools
import math

import jax
import jax.numpy as jnp
from jax import lax
from jax.experimental import pallas as pl
from jax.experimental.pallas import tpu as pltpu
from jax.sharding import PartitionSpec as P

EPSILON = 1e-06
F32 = jnp.float32
BF16 = jnp.bfloat16
N = 16
NT = (((1,), (1,)), ((), ()))
MESH = pl.DeviceIdType.MESH


def ring_peers(me):
    return [lax.rem(me + o, N) for o in range(1, N)]


def signal_all(barrier, ka, pb):
    for peer in ring_peers(ka):
        pl.semaphore_signal(barrier, inc=1, device_id={"ka": peer}, device_id_type=MESH)
    for peer in ring_peers(pb):
        pl.semaphore_signal(barrier, inc=1, device_id={"pb": peer}, device_id_type=MESH)


def send_one(source, target, send_sem, recv_sem, device):
    copy = pltpu.make_async_remote_copy(
        src_ref=source,
        dst_ref=target,
        send_sem=send_sem,
        recv_sem=recv_sem,
        device_id=device,
        device_id_type=MESH,
    )
    copy.start()
    return copy


def recv_one(target, send_sem, recv_sem, device):
    pltpu.make_async_remote_copy(
        src_ref=target,
        dst_ref=target,
        send_sem=send_sem,
        recv_sem=recv_sem,
        device_id=device,
        device_id_type=MESH,
    ).wait_recv()


def send_all(axis, me, source, target, sems):
    return [
        send_one(source(peer), target(me), sems[0].at[o], sems[1].at[me], {axis: peer})
        for o, peer in enumerate(ring_peers(me))
    ]


def recv_all(axis, me, target, sems):
    for o, peer in enumerate(ring_peers(me)):
        recv_one(target(peer), sems[0].at[o], sems[1].at[peer], {axis: peer})


def total(x):
    while x.ndim > 2:
        x = jnp.sum(x, axis=0)
    return jnp.sum(jnp.sum(x, axis=0, keepdims=True), axis=1, keepdims=True)


def stat_rows(values):
    row = lax.broadcasted_iota(jnp.int32, (16, 128), 0)
    block = jnp.zeros((16, 128), F32)
    for i, value in enumerate(values):
        rest = jnp.broadcast_to(value, (16, 128))
        for part in range(3):
            piece = rest.astype(BF16).astype(F32)
            block = jnp.where(row == 3 * i + part, piece, block)
            rest = rest - piece
    return block.astype(BF16)


def read_stat(block, i):
    return block[:, 3 * i : 3 * i + 1] + block[:, 3 * i + 1 : 3 * i + 2] + block[:, 3 * i + 2 : 3 * i + 3]


def pack(values):
    row = lax.broadcasted_iota(jnp.int32, (8, 128), 0)
    block = jnp.zeros((8, 128), F32)
    for i, value in enumerate(values):
        block = jnp.where(row == i, jnp.broadcast_to(value, (8, 128)), block)
    return block


def safe_divide(top, bottom):
    return jnp.where(bottom > 0, top / jnp.where(bottom > 0, bottom, 1.0), 0.0)


def loop(count, body):
    def step(i, carry):
        body(i)
        return carry

    lax.fori_loop(0, count, step, 0)


def haydock_kernel(
    entries, factor,
    window_ref, dip_ref, energy_ref, cond_ref, val_ref, w_ref,
    out_ref,
    grid_ref, index_ref, perm_ref, cond_all, val_all, vv_ref, stage_ref, wt_ref,
    pack_ref, rows_ref, drow_ref, erow_ref, msg_ref, dips_ref, u_ref,
    half_ref, pair_ref, screen_ref, sum_ref, part_ref, first_ref, mine_ref, second_ref,
    after_ref, rests_ref, stat_ref, stats_ref, cut_ref,
    row_s, row_r, few_s, few_r, far_s, far_r, cond_s, cond_r, val_s, val_r, dip_s, dip_r, hop_s, hop_r, w_sem, own_sem,
    a_s, a_r, b_s, b_r, d_s, d_r, e_s, e_r,
):
    ka = lax.axis_index("ka")
    pb = lax.axis_index("pb")
    core = lax.rem(pb, 2)
    chip = pb // 2
    x = lax.rem(chip, 4)
    y = chip // 4
    barrier = pltpu.get_barrier_semaphore()
    signal_all(barrier, ka, pb)

    loads = [
        pltpu.make_async_copy(source, target, own_sem.at[1 + i])
        for i, (source, target) in enumerate(
            [
                (cond_ref, perm_ref.at[0]),
                (dip_ref, pack_ref.at[0]),
                (energy_ref, pack_ref.at[1]),
                (val_ref, val_all.at[pb]),
                (window_ref, grid_ref),
            ]
        )
    ]
    for load in loads:
        load.start()
    own_w = pltpu.make_async_copy(w_ref.at[:, :, core], stage_ref.at[pl.ds(core * 8, 8)], own_sem.at[0])
    own_w.start()
    to = lax.broadcasted_iota(jnp.int32, (64, 64), 0)
    fro = lax.broadcasted_iota(jnp.int32, (64, 64), 1)
    pick = (fro == 2 * lax.rem(to, 32) + to // 32).astype(F32).astype(BF16)
    for load in loads:
        load.wait()
    perm_ref[1] = jnp.dot(pick, perm_ref[0], preferred_element_type=F32).astype(BF16)
    cond_all[y, x, ka] = perm_ref[1]
    rows_ref[pb] = pack_ref[...]
    pl.semaphore_wait(barrier, 2 * (N - 1))

    most = pl.ds(0, 48)
    few = pl.ds(48, 16)
    chips = [lax.rem(chip + o, 8) for o in range(1, 8)]

    def at(which):
        return {"pb": which * 2 + core}

    copies = [
        send_one(perm_ref.at[1, few], cond_all.at[y, x, ka, few], few_s.at[o], few_r.at[chip], at(other))
        for o, other in enumerate(chips)
    ]
    copies += send_all(
        "ka", ka, lambda p: perm_ref.at[1, most], lambda p: cond_all.at[y, x, p, most], (cond_s, cond_r)
    )
    copies += send_all("pb", pb, lambda p: pack_ref, lambda p: rows_ref.at[p], (row_s, row_r))
    sibling = {"pb": pb + 1 - 2 * core}
    w_send = send_one(
        w_ref.at[:, :, 1 - core], stage_ref.at[pl.ds(core * 8, 8)], w_sem.at[0], w_sem.at[1], sibling
    )
    copies += [w_send]
    copies += send_all("pb", pb, lambda p: val_all.at[pb], lambda p: val_all.at[p], (val_s, val_r))

    parts = [lax.rem(x + o, 4) for o in (0, 3, 1, 2)]
    for o, other in enumerate(chips):
        recv_one(cond_all.at[other // 4, lax.rem(other, 4), ka, few], few_s.at[o], few_r.at[other], at(other))

    def send_far(part):
        return send_all(
            "ka", ka,
            lambda p: cond_all.at[:, part, ka, few],
            lambda p: cond_all.at[:, part, p, few],
            (far_s.at[part], far_r.at[part]),
        )

    copies += send_far(parts[0])

    recv_all("ka", ka, lambda p: cond_all.at[y, x, p, most], (cond_s, cond_r))
    lower = pl.ds(0, 8)
    upper = pl.ds(8, 8)
    across = (1 - y) * 4 + x
    steps = [lax.rem(x + o, 4) for o in range(1, 4)]
    block = cond_all.at[y, x, :, most]
    copies += [send_one(block, block, hop_s.at[0], hop_r.at[0], at(across))]
    for o in (0, 2, 1):
        for first, which in ((1, upper), (10, lower)):
            block = cond_all.at[y, x, which, most]
            copies += [send_one(block, block, hop_s.at[first + o], hop_r.at[first + o], at(y * 4 + steps[o]))]

    recv_all("pb", pb, lambda p: rows_ref.at[p], (row_s, row_r))
    for i in range(N):
        drow_ref[2 * i : 2 * i + 2, :] = rows_ref[i, 0]
        erow_ref[2 * i : 2 * i + 2, :] = rows_ref[i, 1]
    drow = drow_ref[...]
    msg_ref[0, 0:32, :] = drow.astype(BF16)
    msg_ref[0, 32:48, :] = stat_rows([total(drow * drow)])
    dips_ref[ka] = msg_ref[0]
    copies += send_all("ka", ka, lambda p: msg_ref.at[0], lambda p: dips_ref.at[p], (dip_s, dip_r))

    for part in parts[1:]:
        copies += send_far(part)

    def table(k):
        mine = grid_ref[k]
        for other in range(N):
            theirs = grid_ref[other]
            shift_one = jnp.bitwise_and(lax.shift_right_logical(mine, 5) - lax.shift_right_logical(theirs, 5), 3)
            shift_two = jnp.bitwise_and(lax.shift_right_logical(mine, 2) - lax.shift_right_logical(theirs, 2), 7)
            shift_three = jnp.bitwise_and(mine - theirs, 3)
            q = (shift_one * 8 + shift_two) * 4 + shift_three
            index_ref[k * N + other] = jnp.where(
                lax.shift_right_logical(q, 4) == chip, jnp.bitwise_and(q, 15), 16
            )

    loop(N, table)

    def turn(q):
        for j in range(8):
            wt_ref[j % 4, q, :, j // 4 * 128 : j // 4 * 128 + 128] = stage_ref[q, j].T

    own_w.wait()
    loop(8, lambda q: turn(core * 8 + q))
    for i in range(4):
        wt_ref[i, 16] = jnp.zeros((128, 256), BF16)
    recv_one(stage_ref.at[pl.ds((1 - core) * 8, 8)], w_sem.at[0], w_sem.at[1], sibling)
    loop(8, lambda q: turn((1 - core) * 8 + q))

    recv_all("pb", pb, lambda p: val_all.at[p], (val_s, val_r))

    def spread(k):
        turned = val_all[k].T
        zero = jnp.zeros_like(turned)
        vv_ref[k] = jnp.concatenate(
            [jnp.concatenate([turned, zero], axis=1), jnp.concatenate([zero, turned], axis=1)], axis=0
        )

    loop(N, spread)
    recv_all("ka", ka, lambda p: dips_ref.at[p], (dip_s, dip_r))

    def start_apply(vector_ref):
        for k in range(N):
            both = lax.dot_general(vv_ref[k], vector_ref[k, 0:32, :], NT, preferred_element_type=F32)
            half_ref[k, :, 0:32] = both[0:128].astype(BF16)
            half_ref[k, :, 32:64] = both[128:256].astype(BF16)
            sum_ref[k] = jnp.zeros((64, 128), F32)

    def columns(part, k):
        return jnp.concatenate([cond_all[0, part, k], cond_all[1, part, k]], axis=1)

    def apply_part(part):
        def screen(k):
            acc = jnp.zeros((128, 256), BF16)
            for other in range(N):
                acc = acc + wt_ref[part, index_ref[k * N + other]] * pair_ref[other]
            screen_ref[k] = acc

        for k in range(N):
            pair_ref[k] = jnp.dot(half_ref[k], columns(part, k), preferred_element_type=F32).astype(BF16)
        loop(N, screen)
        for k in range(N):
            sum_ref[k] += lax.dot_general(columns(part, k), screen_ref[k], NT, preferred_element_type=F32)

    def finish_apply(which):
        for k in range(N):
            both = jnp.concatenate([sum_ref[k, 0:32, :], sum_ref[k, 32:64, :]], axis=1)
            high = both.astype(BF16)
            low = (both - high.astype(F32)).astype(BF16)
            part_ref[which, k] = (
                jnp.dot(high, vv_ref[k], preferred_element_type=F32)
                + jnp.dot(low, vv_ref[k], preferred_element_type=F32)
            ).astype(BF16)

    start_apply(dips_ref)
    recv_one(cond_all.at[1 - y, x, :, most], hop_s.at[0], hop_r.at[0], at(across))
    block = cond_all.at[1 - y, x, lower, most]
    for o in range(3):
        copies.append(send_one(block, block, hop_s.at[4 + o], hop_r.at[4 + o], at(y * 4 + steps[o])))

    def recv_far(part):
        recv_all("ka", ka, lambda p: cond_all.at[:, part, p, few], (far_s.at[part], far_r.at[part]))

    for i, o in enumerate((0, 2, 1)):
        back = parts[1 + i]
        recv_one(cond_all.at[y, back, upper, most], hop_s.at[1 + o], hop_r.at[1 + o], at(y * 4 + back))
        block = cond_all.at[y, back, upper, most]
        copies.append(send_one(block, block, hop_s.at[7 + o], hop_r.at[7 + o], at(across)))
    recv_far(parts[0])
    apply_part(parts[0])
    for i, o in enumerate((0, 2, 1)):
        back = parts[1 + i]
        recv_one(cond_all.at[y, back, lower, most], hop_s.at[10 + o], hop_r.at[10 + o], at(y * 4 + back))
        recv_one(cond_all.at[1 - y, back, lower, most], hop_s.at[4 + o], hop_r.at[4 + o], at(y * 4 + back))
        recv_one(cond_all.at[1 - y, back, upper, most], hop_s.at[7 + o], hop_r.at[7 + o], at(across))
        recv_far(back)
        apply_part(back)
    finish_apply(0)

    def reduce_rows(which):
        new = send_all(
            "ka", ka, lambda p: part_ref.at[which, p], lambda p: first_ref.at[which, p], (a_s.at[which], a_r.at[which])
        )
        first_ref[which, ka] = part_ref[which, ka]
        recv_all("ka", ka, lambda p: first_ref.at[which, p], (a_s.at[which], a_r.at[which]))
        mine_ref[which] = jnp.sum(first_ref[which].astype(F32), axis=0).astype(BF16)
        second_ref[which, pb] = mine_ref[which]
        new += send_all(
            "pb", pb, lambda p: mine_ref.at[which], lambda p: second_ref.at[which, p], (b_s.at[which], b_r.at[which])
        )
        recv_all("pb", pb, lambda p: second_ref.at[which, p], (b_s.at[which], b_r.at[which]))
        return jnp.sum(second_ref[which].astype(F32), axis=0), new

    kernel_row, new = reduce_rows(0)
    copies += new
    squares = read_stat(dips_ref[:, 32:48, :].astype(F32), 0)
    scale = 1.0 / jnp.sqrt(jnp.sum(squares, axis=0) / entries + EPSILON)
    vector = drow_ref[...] * scale
    image = erow_ref[...] * vector - factor * scale * kernel_row
    norm = total(vector * vector)
    inner = total(vector * image)
    slope = safe_divide(inner, norm)
    rest = image - slope * vector
    msg_ref[1, 0:32, :] = rest.astype(BF16)
    msg_ref[1, 32:48, :] = stat_rows([inner, slope, total(rest * rest), norm])
    rests_ref[ka] = msg_ref[1]
    copies += send_all("ka", ka, lambda p: msg_ref.at[1], lambda p: rests_ref.at[p], (d_s, d_r))
    recv_all("ka", ka, lambda p: rests_ref.at[p], (d_s, d_r))
    stats = rests_ref[:, 32:48, :].astype(F32)
    alpha_zero = jnp.sum(read_stat(stats, 0), axis=0) / entries
    off = read_stat(stats, 1) - alpha_zero
    square = jnp.sum(read_stat(stats, 2) + read_stat(stats, 3) * off * off, axis=0) / entries
    beta_zero = jnp.sqrt(square + EPSILON)
    scaled = off * scale
    for k in range(N):
        u_ref[k] = (
            rests_ref[k, 0:32, :].astype(F32) + scaled[k] * dips_ref[k, 0:32, :].astype(F32)
        ).astype(BF16)
    after_ref[0] = vector
    after_ref[1] = (image - alpha_zero * vector) / beta_zero

    start_apply(u_ref)
    loop(4, apply_part)
    finish_apply(1)
    kernel_row, new = reduce_rows(1)
    copies += new
    former = after_ref[0]
    vector = after_ref[1]
    image = erow_ref[...] * vector - factor / beta_zero * kernel_row
    rest = image - beta_zero * former
    norm = total(vector * vector)
    slope = safe_divide(total(vector * rest), norm)
    gap = rest - slope * vector
    stat_ref[...] = pack([total(vector * image), slope, total(gap * gap), norm])
    stats_ref[ka] = stat_ref[...]
    copies += send_all("ka", ka, lambda p: stat_ref, lambda p: stats_ref.at[p], (e_s, e_r))
    recv_all("ka", ka, lambda p: stats_ref.at[p], (e_s, e_r))
    inners, slopes, lefts, norms = [stats_ref[:, i : i + 1, :] for i in range(4)]
    alpha = jnp.sum(inners, axis=0) / entries
    off = slopes - alpha
    beta = jnp.sqrt(jnp.sum(lefts + norms * off * off, axis=0) / entries + EPSILON)
    last = (rest - alpha * vector) / beta
    for i in range(N):
        cut_ref[i] = last[2 * i : 2 * i + 2, :]
    out_ref[0:2, :] = cut_ref[pb]
    lane = lax.broadcasted_iota(jnp.int32, (1, 128), 1)
    out_ref[2:3, :] = jnp.where(
        lane == 0, alpha_zero, jnp.where(lane == 1, alpha, jnp.where(lane == 2, beta_zero, beta))
    )
    for copy in copies:
        copy.wait_send()


def haydock(entries, factor, *args):
    sem = pltpu.SemaphoreType.DMA
    vmem = pl.BlockSpec(memory_space=pltpu.VMEM)
    pair = [sem((N,)), sem((N,))]
    return pl.pallas_call(
        functools.partial(haydock_kernel, entries, factor),
        out_shape=jax.ShapeDtypeStruct((3, 128), F32),
        in_specs=[pl.BlockSpec(memory_space=pltpu.HBM)] * 6,
        out_specs=vmem,
        scratch_shapes=[
            pltpu.SMEM((N,), jnp.int32),
            pltpu.SMEM((N * N,), jnp.int32),
            pltpu.VMEM((2, 64, 128), BF16),
            pltpu.VMEM((2, 4, N, 64, 128), BF16),
            pltpu.VMEM((N, 64, 128), BF16),
            pltpu.VMEM((N, 256, 128), BF16),
            pltpu.VMEM((16, 8, 128, 128), BF16),
            pltpu.VMEM((4, 17, 128, 256), BF16),
            pltpu.VMEM((2, 2, 128), F32),
            pltpu.VMEM((N, 2, 2, 128), F32),
            pltpu.VMEM((32, 128), F32),
            pltpu.VMEM((32, 128), F32),
            pltpu.VMEM((2, 48, 128), BF16),
            pltpu.VMEM((N, 48, 128), BF16),
            pltpu.VMEM((N, 32, 128), BF16),
            pltpu.VMEM((N, 128, 64), BF16),
            pltpu.VMEM((N, 128, 256), BF16),
            pltpu.VMEM((N, 128, 256), BF16),
            pltpu.VMEM((N, 64, 128), F32),
            pltpu.VMEM((2, N, 32, 128), BF16),
            pltpu.VMEM((2, N, 32, 128), BF16),
            pltpu.VMEM((2, 32, 128), BF16),
            pltpu.VMEM((2, N, 32, 128), BF16),
            pltpu.VMEM((2, 32, 128), F32),
            pltpu.VMEM((N, 48, 128), BF16),
            pltpu.VMEM((8, 128), F32),
            pltpu.VMEM((N, 8, 128), F32),
            pltpu.VMEM((N, 2, 128), F32),
        ]
        + pair * 2
        + [sem((4, N)), sem((4, N))]
        + pair * 4
        + [sem((2,)), sem((6,))]
        + [sem((2, N))] * 4
        + pair * 2,
        compiler_params=pltpu.CompilerParams(
            collective_id=0, has_side_effects=True, vmem_limit_bytes=63 * 1024 * 1024
        ),
        name="haydock",
    )(*args)


def per_device(dipole, energy, cond_amp, val_amp, screened, window):
    entries = 16 * 4096
    factor = 1.0 / (2048 * math.sqrt(entries))
    out = haydock(
        entries,
        factor,
        window,
        dipole.reshape(2, 128),
        energy.reshape(2, 128),
        cond_amp[0],
        val_amp[0],
        screened.reshape(8, 8, 2, 128, 128),
    )
    return out[2, :4], out[:2].reshape(1, 256)


def solution(mesh):
    in_specs = (
        P("ka", "pb"),
        P("ka", "pb"),
        P("ka", None, "pb"),
        P("pb", None, "ka"),
        P("pb", None, "ka"),
        P(),
    )
    out_specs = (P(), P("ka", "pb"))
    return jax.shard_map(
        per_device, mesh=mesh, in_specs=in_specs, out_specs=out_specs, check_vma=False
    )
```

```python
import functools
import math

import jax
import jax.numpy as jnp
from jax import lax
from jax.experimental import pallas as pl
from jax.experimental.pallas import tpu as pltpu
from jax.sharding import PartitionSpec as P

EPSILON = 1e-06
F32 = jnp.float32
BF16 = jnp.bfloat16
N = 16
NT = (((1,), (1,)), ((), ()))
MESH = pl.DeviceIdType.MESH


def ring_peers(me):
    return [lax.rem(me + o, N) for o in range(1, N)]


def signal_all(barrier, ka, pb):
    for peer in ring_peers(ka):
        pl.semaphore_signal(barrier, inc=1, device_id={"ka": peer}, device_id_type=MESH)
    for peer in ring_peers(pb):
        pl.semaphore_signal(barrier, inc=1, device_id={"pb": peer}, device_id_type=MESH)


def send_one(source, target, send_sem, recv_sem, device):
    copy = pltpu.make_async_remote_copy(
        src_ref=source,
        dst_ref=target,
        send_sem=send_sem,
        recv_sem=recv_sem,
        device_id=device,
        device_id_type=MESH,
    )
    copy.start()
    return copy


def recv_one(target, send_sem, recv_sem, device):
    pltpu.make_async_remote_copy(
        src_ref=target,
        dst_ref=target,
        send_sem=send_sem,
        recv_sem=recv_sem,
        device_id=device,
        device_id_type=MESH,
    ).wait_recv()


def send_all(axis, me, source, target, sems):
    return [
        send_one(source(peer), target(me), sems[0].at[o], sems[1].at[me], {axis: peer})
        for o, peer in enumerate(ring_peers(me))
    ]


def recv_all(axis, me, target, sems):
    for o, peer in enumerate(ring_peers(me)):
        recv_one(target(peer), sems[0].at[o], sems[1].at[peer], {axis: peer})


def total(x):
    while x.ndim > 2:
        x = jnp.sum(x, axis=0)
    return jnp.sum(jnp.sum(x, axis=0, keepdims=True), axis=1, keepdims=True)


def stat_rows(values):
    row = lax.broadcasted_iota(jnp.int32, (16, 128), 0)
    block = jnp.zeros((16, 128), F32)
    for i, value in enumerate(values):
        rest = jnp.broadcast_to(value, (16, 128))
        for part in range(3):
            piece = rest.astype(BF16).astype(F32)
            block = jnp.where(row == 3 * i + part, piece, block)
            rest = rest - piece
    return block.astype(BF16)


def read_stat(block, i):
    return block[:, 3 * i : 3 * i + 1] + block[:, 3 * i + 1 : 3 * i + 2] + block[:, 3 * i + 2 : 3 * i + 3]


def pack(values):
    lane = lax.broadcasted_iota(jnp.int32, (1, 128), 1)
    block = jnp.zeros((1, 128), F32)
    for i, value in enumerate(values):
        block = jnp.where(lane == i, jnp.broadcast_to(value, (1, 128)), block)
    return block


def safe_divide(top, bottom):
    return jnp.where(bottom > 0, top / jnp.where(bottom > 0, bottom, 1.0), 0.0)


def drain(copies):
    for copy in copies:
        copy.wait_send()


def loop(count, body):
    def step(i, carry):
        body(i)
        return carry

    lax.fori_loop(0, count, step, 0)


def haydock_kernel(
    entries, factor,
    window_ref, dip_ref, energy_ref, cond_ref, val_ref, w_ref,
    out_ref,
    grid_ref, index_ref, perm_ref, cond_all, val_all, vv_ref, stage_ref, wt_ref,
    pack_ref, rows_ref, drow_ref, erow_ref, msg_ref, dips_ref, u_ref,
    half_ref, pair_ref, screen_ref, sum_ref, part_ref, first_ref, mine_ref, second_ref,
    after_ref, rests_ref, stat_ref, stats_ref, cut_ref,
    row_s, row_r, few_s, few_r, far_s, far_r, side_s, side_r, cond_s, cond_r, val_s, val_r, dip_s, dip_r, hop_s, hop_r, w_sem, own_sem,
    a_s, a_r, b_s, b_r, d_s, d_r, e_s, e_r,
):
    ka = lax.axis_index("ka")
    pb = lax.axis_index("pb")
    core = lax.rem(pb, 2)
    chip = pb // 2
    x = lax.rem(chip, 4)
    z = ka // 2
    side = lax.rem(ka, 2)
    y = chip // 4
    barrier = pltpu.get_barrier_semaphore()
    signal_all(barrier, ka, pb)
    mirror = {"ka": ka + 1 - 2 * side, "pb": lax.rem(pb + 8, N)}
    pl.semaphore_signal(barrier, inc=1, device_id=mirror, device_id_type=MESH)

    loads = [
        pltpu.make_async_copy(source, target, own_sem.at[1 + i])
        for i, (source, target) in enumerate(
            [
                (cond_ref, perm_ref.at[0]),
                (dip_ref, pack_ref.at[0]),
                (energy_ref, pack_ref.at[1]),
                (val_ref, val_all.at[pb]),
                (window_ref, grid_ref),
            ]
        )
    ]
    for load in loads:
        load.start()
    own_w = pltpu.make_async_copy(w_ref.at[:, :, core], stage_ref.at[pl.ds(core * 8, 8)], own_sem.at[0])
    own_w.start()
    to = lax.broadcasted_iota(jnp.int32, (64, 64), 0)
    fro = lax.broadcasted_iota(jnp.int32, (64, 64), 1)
    pick = (fro == 2 * lax.rem(to, 32) + to // 32).astype(F32).astype(BF16)
    for load in loads:
        load.wait()
    perm_ref[1] = jnp.dot(pick, perm_ref[0], preferred_element_type=F32).astype(BF16)
    cond_all[y, x, z, side] = perm_ref[1]
    rows_ref[pb] = pack_ref[...]
    pl.semaphore_wait(barrier, 2 * (N - 1) + 1)

    most = pl.ds(0, 48)
    few = pl.ds(48, 16)
    chips = [lax.rem(chip + o, 8) for o in range(1, 8)]

    def at(which):
        return {"pb": which * 2 + core}

    copies = [
        send_one(perm_ref.at[1, few], cond_all.at[y, x, z, side, few], few_s.at[o], few_r.at[chip], at(other))
        for o, other in enumerate(chips)
    ]
    copies += send_all(
        "ka", ka, lambda p: perm_ref.at[1, most], lambda p: cond_all.at[y, x, p // 2, lax.rem(p, 2), most], (cond_s, cond_r)
    )
    copies += send_all("pb", pb, lambda p: pack_ref, lambda p: rows_ref.at[p], (row_s, row_r))
    sibling = {"pb": pb + 1 - 2 * core}
    w_send = send_one(
        w_ref.at[:, :, 1 - core], stage_ref.at[pl.ds(core * 8, 8)], w_sem.at[0], w_sem.at[1], sibling
    )
    copies += [w_send]
    copies += send_all("pb", pb, lambda p: val_all.at[pb], lambda p: val_all.at[p], (val_s, val_r))

    parts = [lax.rem(x + o, 4) for o in (0, 3, 1, 2)]
    for o, other in enumerate(chips):
        recv_one(cond_all.at[other // 4, lax.rem(other, 4), z, side, few], few_s.at[o], few_r.at[other], at(other))

    beside = {"ka": ka + 1 - 2 * side}
    columns_z = [lax.rem(z + o, 8) for o in range(1, 8)]

    def send_far(part):
        block = cond_all.at[:, part, z, side, few]
        return [
            send_one(block, block, far_s.at[part, o], far_r.at[part, z], {"ka": other * 2 + side})
            for o, other in enumerate(columns_z)
        ]

    def pass_far(part):
        for o, other in enumerate(columns_z):
            block = cond_all.at[:, part, other, side, few]
            recv_one(block, far_s.at[part, o], far_r.at[part, other], {"ka": other * 2 + side})
        block = cond_all.at[:, part, :, side, few]
        return [send_one(block, block, side_s.at[part], side_r.at[part], beside)]

    copies += send_far(parts[0])

    recv_all("ka", ka, lambda p: cond_all.at[y, x, p // 2, lax.rem(p, 2), most], (cond_s, cond_r))
    lower = pl.ds(0, 4)
    upper = pl.ds(4, 4)
    steps = [lax.rem(x + o, 4) for o in range(1, 4)]
    block = cond_all.at[y, x, :, :, most]
    copies += [send_one(block, block, hop_s.at[0], hop_r.at[0], mirror)]
    for o in (0, 2, 1):
        for first, which in ((1, upper), (10, lower)):
            block = cond_all.at[y, x, which, :, most]
            copies += [send_one(block, block, hop_s.at[first + o], hop_r.at[first + o], at(y * 4 + steps[o]))]

    recv_all("pb", pb, lambda p: rows_ref.at[p], (row_s, row_r))
    for i in range(N):
        drow_ref[2 * i : 2 * i + 2, :] = rows_ref[i, 0]
        erow_ref[2 * i : 2 * i + 2, :] = rows_ref[i, 1]
    drow = drow_ref[...]
    msg_ref[0, 0:32, :] = drow.astype(BF16)
    msg_ref[0, 32:48, :] = stat_rows([total(drow * drow)])
    dips_ref[ka] = msg_ref[0]
    copies += send_all("ka", ka, lambda p: msg_ref.at[0], lambda p: dips_ref.at[p], (dip_s, dip_r))

    for part in parts[1:]:
        copies += send_far(part)

    def table(k):
        mine = grid_ref[k]
        for other in range(N):
            theirs = grid_ref[other]
            shift_one = jnp.bitwise_and(lax.shift_right_logical(mine, 5) - lax.shift_right_logical(theirs, 5), 3)
            shift_two = jnp.bitwise_and(lax.shift_right_logical(mine, 2) - lax.shift_right_logical(theirs, 2), 7)
            shift_three = jnp.bitwise_and(mine - theirs, 3)
            q = (shift_one * 8 + shift_two) * 4 + shift_three
            index_ref[k * N + other] = jnp.where(
                lax.shift_right_logical(q, 4) == chip, jnp.bitwise_and(q, 15), 16
            )

    loop(N, table)

    def turn(q):
        for j in range(8):
            wt_ref[j % 4, q, :, j // 4 * 128 : j // 4 * 128 + 128] = stage_ref[q, j].T

    own_w.wait()
    loop(8, lambda q: turn(core * 8 + q))
    for i in range(4):
        wt_ref[i, 16] = jnp.zeros((128, 256), BF16)
    recv_one(stage_ref.at[pl.ds((1 - core) * 8, 8)], w_sem.at[0], w_sem.at[1], sibling)
    loop(8, lambda q: turn((1 - core) * 8 + q))

    recv_all("pb", pb, lambda p: val_all.at[p], (val_s, val_r))

    def spread(k):
        turned = val_all[k].T
        zero = jnp.zeros_like(turned)
        vv_ref[k] = jnp.concatenate(
            [jnp.concatenate([turned, zero], axis=1), jnp.concatenate([zero, turned], axis=1)], axis=0
        )

    loop(N, spread)
    recv_all("ka", ka, lambda p: dips_ref.at[p], (dip_s, dip_r))

    def start_apply(vector_ref):
        for k in range(N):
            both = lax.dot_general(vv_ref[k], vector_ref[k, 0:32, :], NT, preferred_element_type=F32)
            half_ref[k, :, 0:32] = both[0:128].astype(BF16)
            half_ref[k, :, 32:64] = both[128:256].astype(BF16)
            sum_ref[k] = jnp.zeros((64, 128), F32)

    def columns(part, k):
        return jnp.concatenate([cond_all[0, part, k // 2, k % 2], cond_all[1, part, k // 2, k % 2]], axis=1)

    def apply_part(part):
        def screen(g):
            for top in (0, 64):
                rows = slice(top, top + 64)
                accs = [jnp.zeros((64, 256), BF16)] * 4
                for other in range(N):
                    pair = pair_ref[other, rows, :]
                    for i in range(4):
                        accs[i] = accs[i] + wt_ref[part, index_ref[(g * 4 + i) * N + other], rows, :] * pair
                for i in range(4):
                    screen_ref[g * 4 + i, rows, :] = accs[i]

        for k in range(N):
            pair_ref[k] = jnp.dot(half_ref[k], columns(part, k), preferred_element_type=F32).astype(BF16)
        loop(N // 4, screen)
        for k in range(N):
            sum_ref[k] += lax.dot_general(columns(part, k), screen_ref[k], NT, preferred_element_type=F32)

    def finish_apply(which):
        for k in range(N):
            both = jnp.concatenate([sum_ref[k, 0:32, :], sum_ref[k, 32:64, :]], axis=1)
            high = both.astype(BF16)
            low = (both - high.astype(F32)).astype(BF16)
            part_ref[which, k] = (
                jnp.dot(high, vv_ref[k], preferred_element_type=F32)
                + jnp.dot(low, vv_ref[k], preferred_element_type=F32)
            ).astype(BF16)

    start_apply(dips_ref)
    for part in parts[:2]:
        copies += pass_far(part)
    recv_one(cond_all.at[1 - y, x, :, :, most], hop_s.at[0], hop_r.at[0], mirror)
    block = cond_all.at[1 - y, x, lower, :, most]
    for o in range(3):
        copies.append(send_one(block, block, hop_s.at[4 + o], hop_r.at[4 + o], at(y * 4 + steps[o])))

    def recv_far(part):
        recv_one(cond_all.at[:, part, :, 1 - side, few], side_s.at[part], side_r.at[part], beside)

    for i, o in enumerate((0, 2, 1)):
        near = parts[1 + i]
        recv_one(cond_all.at[y, near, upper, :, most], hop_s.at[1 + o], hop_r.at[1 + o], at(y * 4 + near))
        block = cond_all.at[y, near, upper, :, most]
        copies.append(send_one(block, block, hop_s.at[7 + o], hop_r.at[7 + o], mirror))
    for part in parts[2:]:
        copies += pass_far(part)
    recv_far(parts[0])
    apply_part(parts[0])
    for i, o in enumerate((0, 2, 1)):
        near = parts[1 + i]
        recv_one(cond_all.at[y, near, lower, :, most], hop_s.at[10 + o], hop_r.at[10 + o], at(y * 4 + near))
        recv_one(cond_all.at[1 - y, near, lower, :, most], hop_s.at[4 + o], hop_r.at[4 + o], at(y * 4 + near))
        recv_one(cond_all.at[1 - y, near, upper, :, most], hop_s.at[7 + o], hop_r.at[7 + o], mirror)
        recv_far(near)
        apply_part(near)
    finish_apply(0)

    def reduce_rows(which, before):
        new = send_all(
            "ka", ka, lambda p: part_ref.at[which, p], lambda p: first_ref.at[which, p], (a_s.at[which], a_r.at[which])
        )
        first_ref[which, ka] = part_ref[which, ka]
        drain(before)
        recv_all("ka", ka, lambda p: first_ref.at[which, p], (a_s.at[which], a_r.at[which]))
        mine_ref[which] = jnp.sum(first_ref[which].astype(F32), axis=0).astype(BF16)
        second_ref[which, pb] = mine_ref[which]
        last = send_all(
            "pb", pb, lambda p: mine_ref.at[which], lambda p: second_ref.at[which, p], (b_s.at[which], b_r.at[which])
        )
        drain(new)
        recv_all("pb", pb, lambda p: second_ref.at[which, p], (b_s.at[which], b_r.at[which]))
        return jnp.sum(second_ref[which].astype(F32), axis=0), last

    kernel_row, copies = reduce_rows(0, copies)
    squares = read_stat(dips_ref[:, 32:48, :].astype(F32), 0)
    scale = 1.0 / jnp.sqrt(jnp.sum(squares, axis=0) / entries + EPSILON)
    vector = drow_ref[...] * scale
    image = erow_ref[...] * vector - factor * scale * kernel_row
    norm = total(vector * vector)
    inner = total(vector * image)
    slope = safe_divide(inner, norm)
    rest = image - slope * vector
    msg_ref[1, 0:32, :] = rest.astype(BF16)
    msg_ref[1, 32:48, :] = stat_rows([inner, slope, total(rest * rest), norm])
    rests_ref[ka] = msg_ref[1]
    copies += send_all("ka", ka, lambda p: msg_ref.at[1], lambda p: rests_ref.at[p], (d_s, d_r))
    recv_all("ka", ka, lambda p: rests_ref.at[p], (d_s, d_r))
    stats = rests_ref[:, 32:48, :].astype(F32)
    alpha_zero = jnp.sum(read_stat(stats, 0), axis=0) / entries
    off = read_stat(stats, 1) - alpha_zero
    square = jnp.sum(read_stat(stats, 2) + read_stat(stats, 3) * off * off, axis=0) / entries
    beta_zero = jnp.sqrt(square + EPSILON)
    scaled = off * scale
    for k in range(N):
        u_ref[k] = (
            rests_ref[k, 0:32, :].astype(F32) + scaled[k] * dips_ref[k, 0:32, :].astype(F32)
        ).astype(BF16)
    after_ref[0] = vector
    after_ref[1] = (image - alpha_zero * vector) / beta_zero

    start_apply(u_ref)
    for part in range(4):
        apply_part(part)
    finish_apply(1)
    kernel_row, copies = reduce_rows(1, copies)
    former = after_ref[0]
    vector = after_ref[1]
    image = erow_ref[...] * vector - factor / beta_zero * kernel_row
    rest = image - beta_zero * former
    norm = total(vector * vector)
    slope = safe_divide(total(vector * rest), norm)
    gap = rest - slope * vector
    stat_ref[...] = pack([total(vector * image), slope, total(gap * gap), norm])
    stats_ref[ka] = stat_ref[...]
    final = send_all("ka", ka, lambda p: stat_ref, lambda p: stats_ref.at[p], (e_s, e_r))
    drain(copies)
    recv_all("ka", ka, lambda p: stats_ref.at[p], (e_s, e_r))
    stats = stats_ref[...]
    inners, slopes, lefts, norms = [
        jnp.broadcast_to(stats[:, :, i : i + 1], (N, 1, 128)) for i in range(4)
    ]
    alpha = jnp.sum(inners, axis=0) / entries
    off = slopes - alpha
    beta = jnp.sqrt(jnp.sum(lefts + norms * off * off, axis=0) / entries + EPSILON)
    last = (rest - alpha * vector) / beta
    for i in range(N):
        cut_ref[i] = last[2 * i : 2 * i + 2, :]
    out_ref[0:2, :] = cut_ref[pb]
    lane = lax.broadcasted_iota(jnp.int32, (1, 128), 1)
    out_ref[2:3, :] = jnp.where(
        lane == 0, alpha_zero, jnp.where(lane == 1, alpha, jnp.where(lane == 2, beta_zero, beta))
    )
    drain(final)


def haydock(entries, factor, *args):
    sem = pltpu.SemaphoreType.DMA
    vmem = pl.BlockSpec(memory_space=pltpu.VMEM)
    pair = [sem((N,)), sem((N,))]
    return pl.pallas_call(
        functools.partial(haydock_kernel, entries, factor),
        out_shape=jax.ShapeDtypeStruct((3, 128), F32),
        in_specs=[pl.BlockSpec(memory_space=pltpu.HBM)] * 6,
        out_specs=vmem,
        scratch_shapes=[
            pltpu.SMEM((N,), jnp.int32),
            pltpu.SMEM((N * N,), jnp.int32),
            pltpu.VMEM((2, 64, 128), BF16),
            pltpu.VMEM((2, 4, 8, 2, 64, 128), BF16),
            pltpu.VMEM((N, 64, 128), BF16),
            pltpu.VMEM((N, 256, 128), BF16),
            pltpu.VMEM((16, 8, 128, 128), BF16),
            pltpu.VMEM((4, 17, 128, 256), BF16),
            pltpu.VMEM((2, 2, 128), F32),
            pltpu.VMEM((N, 2, 2, 128), F32),
            pltpu.VMEM((32, 128), F32),
            pltpu.VMEM((32, 128), F32),
            pltpu.VMEM((2, 48, 128), BF16),
            pltpu.VMEM((N, 48, 128), BF16),
            pltpu.VMEM((N, 32, 128), BF16),
            pltpu.VMEM((N, 128, 64), BF16),
            pltpu.VMEM((N, 128, 256), BF16),
            pltpu.VMEM((N, 128, 256), BF16),
            pltpu.VMEM((N, 64, 128), F32),
            pltpu.VMEM((2, N, 32, 128), BF16),
            pltpu.VMEM((2, N, 32, 128), BF16),
            pltpu.VMEM((2, 32, 128), BF16),
            pltpu.VMEM((2, N, 32, 128), BF16),
            pltpu.VMEM((2, 32, 128), F32),
            pltpu.VMEM((N, 48, 128), BF16),
            pltpu.VMEM((1, 128), F32),
            pltpu.VMEM((N, 1, 128), F32),
            pltpu.VMEM((N, 2, 128), F32),
        ]
        + pair * 2
        + [sem((4, N)), sem((4, N)), sem((4,)), sem((4,))]
        + pair * 4
        + [sem((2,)), sem((6,))]
        + [sem((2, N))] * 4
        + pair * 2,
        compiler_params=pltpu.CompilerParams(
            collective_id=0, has_side_effects=True, vmem_limit_bytes=63 * 1024 * 1024
        ),
        name="haydock",
    )(*args)


def per_device(dipole, energy, cond_amp, val_amp, screened, window):
    entries = 16 * 4096
    factor = 1.0 / (2048 * math.sqrt(entries))
    out = haydock(
        entries,
        factor,
        window,
        dipole.reshape(2, 128),
        energy.reshape(2, 128),
        cond_amp[0],
        val_amp[0],
        screened.reshape(8, 8, 2, 128, 128),
    )
    return out[2, :4], out[:2].reshape(1, 256)


def solution(mesh):
    in_specs = (
        P("ka", "pb"),
        P("ka", "pb"),
        P("ka", None, "pb"),
        P("pb", None, "ka"),
        P("pb", None, "ka"),
        P(),
    )
    out_specs = (P(), P("ka", "pb"))
    return jax.shard_map(
        per_device, mesh=mesh, in_specs=in_specs, out_specs=out_specs, check_vma=False
    )
```

```python
import functools
import math

import jax
import jax.numpy as jnp
from jax import lax
from jax.experimental import pallas as pl
from jax.experimental.pallas import tpu as pltpu
from jax.sharding import PartitionSpec as P

EPSILON = 1e-06
F32 = jnp.float32
BF16 = jnp.bfloat16
N = 16
NT = (((1,), (1,)), ((), ()))
MESH = pl.DeviceIdType.MESH


def ring_peers(me):
    return [lax.rem(me + o, N) for o in range(1, N)]


def signal_all(barrier, ka, pb):
    for peer in ring_peers(ka):
        pl.semaphore_signal(barrier, inc=1, device_id={"ka": peer}, device_id_type=MESH)
    for peer in ring_peers(pb):
        pl.semaphore_signal(barrier, inc=1, device_id={"pb": peer}, device_id_type=MESH)


def send_one(source, target, send_sem, recv_sem, device):
    copy = pltpu.make_async_remote_copy(
        src_ref=source,
        dst_ref=target,
        send_sem=send_sem,
        recv_sem=recv_sem,
        device_id=device,
        device_id_type=MESH,
    )
    copy.start()
    return copy


def recv_one(target, send_sem, recv_sem, device):
    pltpu.make_async_remote_copy(
        src_ref=target,
        dst_ref=target,
        send_sem=send_sem,
        recv_sem=recv_sem,
        device_id=device,
        device_id_type=MESH,
    ).wait_recv()


def send_all(axis, me, source, target, sems):
    return [
        send_one(source(peer), target(me), sems[0].at[o], sems[1].at[me], {axis: peer})
        for o, peer in enumerate(ring_peers(me))
    ]


def recv_all(axis, me, target, sems):
    for o, peer in enumerate(ring_peers(me)):
        recv_one(target(peer), sems[0].at[o], sems[1].at[peer], {axis: peer})


def total(x):
    while x.ndim > 2:
        x = jnp.sum(x, axis=0)
    return jnp.sum(jnp.sum(x, axis=0, keepdims=True), axis=1, keepdims=True)


def stat_rows(values):
    row = lax.broadcasted_iota(jnp.int32, (16, 128), 0)
    block = jnp.zeros((16, 128), F32)
    for i, value in enumerate(values):
        rest = jnp.broadcast_to(value, (16, 128))
        for part in range(3):
            piece = rest.astype(BF16).astype(F32)
            block = jnp.where(row == 3 * i + part, piece, block)
            rest = rest - piece
    return block.astype(BF16)


def read_stat(block, i):
    return block[:, 3 * i : 3 * i + 1] + block[:, 3 * i + 1 : 3 * i + 2] + block[:, 3 * i + 2 : 3 * i + 3]


def pack(values):
    lane = lax.broadcasted_iota(jnp.int32, (1, 128), 1)
    block = jnp.zeros((1, 128), F32)
    for i, value in enumerate(values):
        block = jnp.where(lane == i, jnp.broadcast_to(value, (1, 128)), block)
    return block


def safe_divide(top, bottom):
    return jnp.where(bottom > 0, top / jnp.where(bottom > 0, bottom, 1.0), 0.0)


def drain(copies):
    for copy in copies:
        copy.wait_send()


def loop(count, body):
    def step(i, carry):
        body(i)
        return carry

    lax.fori_loop(0, count, step, 0)


def haydock_kernel(
    entries, factor,
    window_ref, dip_ref, energy_ref, cond_ref, val_ref, w_ref,
    out_ref,
    grid_ref, index_ref, perm_ref, cond_all, val_all, vv_ref, stage_ref, wt_ref,
    pack_ref, rows_ref, drow_ref, erow_ref, msg_ref, dips_ref, u_ref,
    half_ref, pair_ref, screen_ref, sum_ref, part_ref, first_ref, mine_ref, second_ref,
    after_ref, rests_ref, stat_ref, stats_ref, cut_ref,
    row_s, row_r, few_s, few_r, far_s, far_r, side_s, side_r, cond_s, cond_r, val_s, val_r, dip_s, dip_r, hop_s, hop_r, w_sem, own_sem,
    a_s, a_r, b_s, b_r, d_s, d_r, e_s, e_r,
):
    ka = lax.axis_index("ka")
    pb = lax.axis_index("pb")
    core = lax.rem(pb, 2)
    chip = pb // 2
    x = lax.rem(chip, 4)
    z = ka // 2
    side = lax.rem(ka, 2)
    y = chip // 4
    barrier = pltpu.get_barrier_semaphore()
    signal_all(barrier, ka, pb)
    mirror = {"ka": ka + 1 - 2 * side, "pb": lax.rem(pb + 8, N)}
    pl.semaphore_signal(barrier, inc=1, device_id=mirror, device_id_type=MESH)

    loads = [
        pltpu.make_async_copy(source, target, own_sem.at[1 + i])
        for i, (source, target) in enumerate(
            [
                (cond_ref, perm_ref.at[0]),
                (dip_ref, pack_ref.at[0]),
                (energy_ref, pack_ref.at[1]),
                (val_ref, val_all.at[pb]),
                (window_ref, grid_ref),
            ]
        )
    ]
    for load in loads:
        load.start()
    own_w = pltpu.make_async_copy(w_ref.at[:, :, core], stage_ref.at[pl.ds(core * 8, 8)], own_sem.at[0])
    own_w.start()
    to = lax.broadcasted_iota(jnp.int32, (64, 64), 0)
    fro = lax.broadcasted_iota(jnp.int32, (64, 64), 1)
    pick = (fro == 2 * lax.rem(to, 32) + to // 32).astype(F32).astype(BF16)
    for load in loads:
        load.wait()
    perm_ref[1] = jnp.dot(pick, perm_ref[0], preferred_element_type=F32).astype(BF16)
    cond_all[y, x, z, side] = perm_ref[1]
    rows_ref[pb] = pack_ref[...]
    def table(k):
        mine = grid_ref[k]
        for other in range(N):
            theirs = grid_ref[other]
            shift_one = jnp.bitwise_and(lax.shift_right_logical(mine, 5) - lax.shift_right_logical(theirs, 5), 3)
            shift_two = jnp.bitwise_and(lax.shift_right_logical(mine, 2) - lax.shift_right_logical(theirs, 2), 7)
            shift_three = jnp.bitwise_and(mine - theirs, 3)
            q = (shift_one * 8 + shift_two) * 4 + shift_three
            index_ref[k * N + other] = jnp.where(
                lax.shift_right_logical(q, 4) == chip, jnp.bitwise_and(q, 15), 16
            )

    loop(N, table)
    def turn(q):
        for j in range(8):
            wt_ref[j % 4, q, :, j // 4 * 128 : j // 4 * 128 + 128] = stage_ref[q, j].T

    own_w.wait()
    loop(8, lambda q: turn(core * 8 + q))
    for i in range(4):
        wt_ref[i, 16] = jnp.zeros((128, 256), BF16)
    pl.semaphore_wait(barrier, 2 * (N - 1) + 1)

    most = pl.ds(0, 48)
    few = pl.ds(48, 16)
    chips = [lax.rem(chip + o, 8) for o in range(1, 8)]

    def at(which):
        return {"pb": which * 2 + core}

    copies = [
        send_one(perm_ref.at[1, few], cond_all.at[y, x, z, side, few], few_s.at[o], few_r.at[chip], at(other))
        for o, other in enumerate(chips)
    ]
    copies += send_all(
        "ka", ka, lambda p: perm_ref.at[1, most], lambda p: cond_all.at[y, x, p // 2, lax.rem(p, 2), most], (cond_s, cond_r)
    )
    copies += send_all("pb", pb, lambda p: pack_ref, lambda p: rows_ref.at[p], (row_s, row_r))
    sibling = {"pb": pb + 1 - 2 * core}
    w_send = send_one(
        w_ref.at[:, :, 1 - core], stage_ref.at[pl.ds(core * 8, 8)], w_sem.at[0], w_sem.at[1], sibling
    )
    copies += [w_send]
    copies += send_all("pb", pb, lambda p: val_all.at[pb], lambda p: val_all.at[p], (val_s, val_r))

    parts = [lax.rem(x + o, 4) for o in (0, 3, 1, 2)]
    for o, other in enumerate(chips):
        recv_one(cond_all.at[other // 4, lax.rem(other, 4), z, side, few], few_s.at[o], few_r.at[other], at(other))

    beside = {"ka": ka + 1 - 2 * side}
    columns_z = [lax.rem(z + o, 8) for o in range(1, 8)]

    def send_far(part):
        block = cond_all.at[:, part, z, side, few]
        return [
            send_one(block, block, far_s.at[part, o], far_r.at[part, z], {"ka": other * 2 + side})
            for o, other in enumerate(columns_z)
        ]

    def pass_far(part):
        for o, other in enumerate(columns_z):
            block = cond_all.at[:, part, other, side, few]
            recv_one(block, far_s.at[part, o], far_r.at[part, other], {"ka": other * 2 + side})
        block = cond_all.at[:, part, :, side, few]
        return [send_one(block, block, side_s.at[part], side_r.at[part], beside)]

    for part in parts:
        copies += send_far(part)

    recv_all("ka", ka, lambda p: cond_all.at[y, x, p // 2, lax.rem(p, 2), most], (cond_s, cond_r))
    lower = pl.ds(0, 4)
    upper = pl.ds(4, 4)
    steps = [lax.rem(x + o, 4) for o in range(1, 4)]
    block = cond_all.at[y, x, :, :, most]
    copies += [send_one(block, block, hop_s.at[0], hop_r.at[0], mirror)]
    for o, slot, which in ((0, 1, upper), (2, 12, lower), (0, 10, lower), (2, 3, upper)):
        block = cond_all.at[y, x, which, :, most]
        copies += [send_one(block, block, hop_s.at[slot], hop_r.at[slot], at(y * 4 + steps[o]))]

    recv_all("pb", pb, lambda p: rows_ref.at[p], (row_s, row_r))
    for i in range(N):
        drow_ref[2 * i : 2 * i + 2, :] = rows_ref[i, 0]
        erow_ref[2 * i : 2 * i + 2, :] = rows_ref[i, 1]
    drow = drow_ref[...]
    msg_ref[0, 0:32, :] = drow.astype(BF16)
    msg_ref[0, 32:48, :] = stat_rows([total(drow * drow)])
    dips_ref[ka] = msg_ref[0]
    copies += send_all("ka", ka, lambda p: msg_ref.at[0], lambda p: dips_ref.at[p], (dip_s, dip_r))

    for o, slot, which, onward in ((0, 1, upper, 2), (2, 12, lower, 11)):
        near = steps[2 - o]
        block = cond_all.at[y, near, which, :, most]
        recv_one(block, hop_s.at[slot], hop_r.at[slot], at(y * 4 + near))
        copies += [send_one(block, block, hop_s.at[onward], hop_r.at[onward], at(y * 4 + steps[o]))]


    recv_one(stage_ref.at[pl.ds((1 - core) * 8, 8)], w_sem.at[0], w_sem.at[1], sibling)
    loop(8, lambda q: turn((1 - core) * 8 + q))

    for part in parts:
        copies += pass_far(part)
    recv_all("pb", pb, lambda p: val_all.at[p], (val_s, val_r))

    def spread(k):
        turned = val_all[k].T
        zero = jnp.zeros_like(turned)
        vv_ref[k] = jnp.concatenate(
            [jnp.concatenate([turned, zero], axis=1), jnp.concatenate([zero, turned], axis=1)], axis=0
        )

    loop(N, spread)
    recv_all("ka", ka, lambda p: dips_ref.at[p], (dip_s, dip_r))

    def start_apply(vector_ref):
        for k in range(N):
            both = lax.dot_general(vv_ref[k], vector_ref[k, 0:32, :], NT, preferred_element_type=F32)
            half_ref[k, :, 0:32] = both[0:128].astype(BF16)
            half_ref[k, :, 32:64] = both[128:256].astype(BF16)
            sum_ref[k] = jnp.zeros((64, 128), F32)

    def columns(part, k):
        return jnp.concatenate([cond_all[0, part, k // 2, k % 2], cond_all[1, part, k // 2, k % 2]], axis=1)

    def apply_part(part):
        def screen(g):
            for top in (0, 64):
                rows = slice(top, top + 64)
                accs = [jnp.zeros((64, 256), BF16)] * 4
                for other in range(N):
                    pair = pair_ref[other, rows, :]
                    for i in range(4):
                        accs[i] = accs[i] + wt_ref[part, index_ref[(g * 4 + i) * N + other], rows, :] * pair
                for i in range(4):
                    screen_ref[g * 4 + i, rows, :] = accs[i]

        for k in range(N):
            pair_ref[k] = jnp.dot(half_ref[k], columns(part, k), preferred_element_type=F32).astype(BF16)
        for g in range(N // 4):
            screen(g)
        for k in range(N):
            sum_ref[k] += lax.dot_general(columns(part, k), screen_ref[k], NT, preferred_element_type=F32)

    def finish_apply(which):
        for k in range(N):
            both = jnp.concatenate([sum_ref[k, 0:32, :], sum_ref[k, 32:64, :]], axis=1)
            high = both.astype(BF16)
            low = (both - high.astype(F32)).astype(BF16)
            part_ref[which, k] = (
                jnp.dot(high, vv_ref[k], preferred_element_type=F32)
                + jnp.dot(low, vv_ref[k], preferred_element_type=F32)
            ).astype(BF16)

    start_apply(dips_ref)
    recv_one(cond_all.at[1 - y, x, :, :, most], hop_s.at[0], hop_r.at[0], mirror)
    block = cond_all.at[1 - y, x, lower, :, most]
    for o in range(3):
        copies.append(send_one(block, block, hop_s.at[4 + o], hop_r.at[4 + o], at(y * 4 + steps[o])))

    def recv_far(part):
        recv_one(cond_all.at[:, part, :, 1 - side, few], side_s.at[part], side_r.at[part], beside)

    for i, o in enumerate((0, 2, 1)):
        near = parts[1 + i]
        if o != 0:
            recv_one(cond_all.at[y, near, upper, :, most], hop_s.at[1 + o], hop_r.at[1 + o], at(y * 4 + near))
        block = cond_all.at[y, near, upper, :, most]
        copies.append(send_one(block, block, hop_s.at[7 + o], hop_r.at[7 + o], mirror))
    recv_far(parts[0])
    apply_part(parts[0])
    for i, o in enumerate((0, 2, 1)):
        near = parts[1 + i]
        if o != 2:
            recv_one(cond_all.at[y, near, lower, :, most], hop_s.at[10 + o], hop_r.at[10 + o], at(y * 4 + near))
        recv_one(cond_all.at[1 - y, near, lower, :, most], hop_s.at[4 + o], hop_r.at[4 + o], at(y * 4 + near))
        recv_one(cond_all.at[1 - y, near, upper, :, most], hop_s.at[7 + o], hop_r.at[7 + o], mirror)
        recv_far(near)
        apply_part(near)
    finish_apply(0)

    def reduce_rows(which, before):
        new = send_all(
            "ka", ka, lambda p: part_ref.at[which, p], lambda p: first_ref.at[which, p], (a_s.at[which], a_r.at[which])
        )
        first_ref[which, ka] = part_ref[which, ka]
        drain(before)
        recv_all("ka", ka, lambda p: first_ref.at[which, p], (a_s.at[which], a_r.at[which]))
        mine_ref[which] = jnp.sum(first_ref[which].astype(F32), axis=0).astype(BF16)
        second_ref[which, pb] = mine_ref[which]
        last = send_all(
            "pb", pb, lambda p: mine_ref.at[which], lambda p: second_ref.at[which, p], (b_s.at[which], b_r.at[which])
        )
        drain(new)
        recv_all("pb", pb, lambda p: second_ref.at[which, p], (b_s.at[which], b_r.at[which]))
        return jnp.sum(second_ref[which].astype(F32), axis=0), last

    kernel_row, copies = reduce_rows(0, copies)
    squares = read_stat(dips_ref[:, 32:48, :].astype(F32), 0)
    scale = 1.0 / jnp.sqrt(jnp.sum(squares, axis=0) / entries + EPSILON)
    vector = drow_ref[...] * scale
    image = erow_ref[...] * vector - factor * scale * kernel_row
    norm = total(vector * vector)
    inner = total(vector * image)
    slope = safe_divide(inner, norm)
    rest = image - slope * vector
    msg_ref[1, 0:32, :] = rest.astype(BF16)
    msg_ref[1, 32:48, :] = stat_rows([inner, slope, total(rest * rest), norm])
    rests_ref[ka] = msg_ref[1]
    copies += send_all("ka", ka, lambda p: msg_ref.at[1], lambda p: rests_ref.at[p], (d_s, d_r))
    recv_all("ka", ka, lambda p: rests_ref.at[p], (d_s, d_r))
    stats = rests_ref[:, 32:48, :].astype(F32)
    alpha_zero = jnp.sum(read_stat(stats, 0), axis=0) / entries
    off = read_stat(stats, 1) - alpha_zero
    square = jnp.sum(read_stat(stats, 2) + read_stat(stats, 3) * off * off, axis=0) / entries
    beta_zero = jnp.sqrt(square + EPSILON)
    scaled = off * scale
    for k in range(N):
        u_ref[k] = (
            rests_ref[k, 0:32, :].astype(F32) + scaled[k] * dips_ref[k, 0:32, :].astype(F32)
        ).astype(BF16)
    after_ref[0] = vector
    after_ref[1] = (image - alpha_zero * vector) / beta_zero

    start_apply(u_ref)
    for part in range(4):
        apply_part(part)
    finish_apply(1)
    kernel_row, copies = reduce_rows(1, copies)
    former = after_ref[0]
    vector = after_ref[1]
    image = erow_ref[...] * vector - factor / beta_zero * kernel_row
    rest = image - beta_zero * former
    norm = total(vector * vector)
    slope = safe_divide(total(vector * rest), norm)
    gap = rest - slope * vector
    stat_ref[...] = pack([total(vector * image), slope, total(gap * gap), norm])
    stats_ref[ka] = stat_ref[...]
    final = send_all("ka", ka, lambda p: stat_ref, lambda p: stats_ref.at[p], (e_s, e_r))
    drain(copies)
    recv_all("ka", ka, lambda p: stats_ref.at[p], (e_s, e_r))
    stats = stats_ref[...]
    inners, slopes, lefts, norms = [
        jnp.broadcast_to(stats[:, :, i : i + 1], (N, 1, 128)) for i in range(4)
    ]
    alpha = jnp.sum(inners, axis=0) / entries
    off = slopes - alpha
    beta = jnp.sqrt(jnp.sum(lefts + norms * off * off, axis=0) / entries + EPSILON)
    last = (rest - alpha * vector) / beta
    for i in range(N):
        cut_ref[i] = last[2 * i : 2 * i + 2, :]
    out_ref[0:2, :] = cut_ref[pb]
    lane = lax.broadcasted_iota(jnp.int32, (1, 128), 1)
    out_ref[2:3, :] = jnp.where(
        lane == 0, alpha_zero, jnp.where(lane == 1, alpha, jnp.where(lane == 2, beta_zero, beta))
    )
    drain(final)


def haydock(entries, factor, *args):
    sem = pltpu.SemaphoreType.DMA
    vmem = pl.BlockSpec(memory_space=pltpu.VMEM)
    pair = [sem((N,)), sem((N,))]
    return pl.pallas_call(
        functools.partial(haydock_kernel, entries, factor),
        out_shape=jax.ShapeDtypeStruct((3, 128), F32),
        in_specs=[pl.BlockSpec(memory_space=pltpu.HBM)] * 6,
        out_specs=vmem,
        scratch_shapes=[
            pltpu.SMEM((N,), jnp.int32),
            pltpu.SMEM((N * N,), jnp.int32),
            pltpu.VMEM((2, 64, 128), BF16),
            pltpu.VMEM((2, 4, 8, 2, 64, 128), BF16),
            pltpu.VMEM((N, 64, 128), BF16),
            pltpu.VMEM((N, 256, 128), BF16),
            pltpu.VMEM((16, 8, 128, 128), BF16),
            pltpu.VMEM((4, 17, 128, 256), BF16),
            pltpu.VMEM((2, 2, 128), F32),
            pltpu.VMEM((N, 2, 2, 128), F32),
            pltpu.VMEM((32, 128), F32),
            pltpu.VMEM((32, 128), F32),
            pltpu.VMEM((2, 48, 128), BF16),
            pltpu.VMEM((N, 48, 128), BF16),
            pltpu.VMEM((N, 32, 128), BF16),
            pltpu.VMEM((N, 128, 64), BF16),
            pltpu.VMEM((N, 128, 256), BF16),
            pltpu.VMEM((N, 128, 256), BF16),
            pltpu.VMEM((N, 64, 128), F32),
            pltpu.VMEM((2, N, 32, 128), BF16),
            pltpu.VMEM((2, N, 32, 128), BF16),
            pltpu.VMEM((2, 32, 128), BF16),
            pltpu.VMEM((2, N, 32, 128), BF16),
            pltpu.VMEM((2, 32, 128), F32),
            pltpu.VMEM((N, 48, 128), BF16),
            pltpu.VMEM((1, 128), F32),
            pltpu.VMEM((N, 1, 128), F32),
            pltpu.VMEM((N, 2, 128), F32),
        ]
        + pair * 2
        + [sem((4, N)), sem((4, N)), sem((4,)), sem((4,))]
        + pair * 4
        + [sem((2,)), sem((6,))]
        + [sem((2, N))] * 4
        + pair * 2,
        compiler_params=pltpu.CompilerParams(
            collective_id=0, has_side_effects=True, vmem_limit_bytes=63 * 1024 * 1024
        ),
        name="haydock",
    )(*args)


def per_device(dipole, energy, cond_amp, val_amp, screened, window):
    entries = 16 * 4096
    factor = 1.0 / (2048 * math.sqrt(entries))
    out = haydock(
        entries,
        factor,
        window,
        dipole.reshape(2, 128),
        energy.reshape(2, 128),
        cond_amp[0],
        val_amp[0],
        screened.reshape(8, 8, 2, 128, 128),
    )
    return out[2, :4], out[:2].reshape(1, 256)


def solution(mesh):
    in_specs = (
        P("ka", "pb"),
        P("ka", "pb"),
        P("ka", None, "pb"),
        P("pb", None, "ka"),
        P("pb", None, "ka"),
        P(),
    )
    out_specs = (P(), P("ka", "pb"))
    return jax.shard_map(
        per_device, mesh=mesh, in_specs=in_specs, out_specs=out_specs, check_vma=False
    )
```

```python
import functools
import math

import jax
import jax.numpy as jnp
from jax import lax
from jax.experimental import pallas as pl
from jax.experimental.pallas import tpu as pltpu
from jax.sharding import PartitionSpec as P

EPSILON = 1e-06
F32 = jnp.float32
BF16 = jnp.bfloat16
N = 16
NT = (((1,), (1,)), ((), ()))
MESH = pl.DeviceIdType.MESH


def ring_peers(me):
    return [lax.rem(me + o, N) for o in range(1, N)]


def signal_all(barrier, ka, pb):
    for peer in ring_peers(ka):
        pl.semaphore_signal(barrier, inc=1, device_id={"ka": peer}, device_id_type=MESH)
    for peer in ring_peers(pb):
        pl.semaphore_signal(barrier, inc=1, device_id={"pb": peer}, device_id_type=MESH)


def send_one(source, target, send_sem, recv_sem, device):
    copy = pltpu.make_async_remote_copy(
        src_ref=source,
        dst_ref=target,
        send_sem=send_sem,
        recv_sem=recv_sem,
        device_id=device,
        device_id_type=MESH,
    )
    copy.start()
    return copy


def recv_one(target, send_sem, recv_sem, device):
    pltpu.make_async_remote_copy(
        src_ref=target,
        dst_ref=target,
        send_sem=send_sem,
        recv_sem=recv_sem,
        device_id=device,
        device_id_type=MESH,
    ).wait_recv()


def send_all(axis, me, source, target, sems):
    return [
        send_one(source(peer), target(me), sems[0].at[o], sems[1].at[me], {axis: peer})
        for o, peer in enumerate(ring_peers(me))
    ]


def recv_all(axis, me, target, sems):
    for o, peer in enumerate(ring_peers(me)):
        recv_one(target(peer), sems[0].at[o], sems[1].at[peer], {axis: peer})


def total(x):
    while x.ndim > 2:
        x = jnp.sum(x, axis=0)
    return jnp.sum(jnp.sum(x, axis=0, keepdims=True), axis=1, keepdims=True)


def stat_rows(values):
    row = lax.broadcasted_iota(jnp.int32, (16, 128), 0)
    block = jnp.zeros((16, 128), F32)
    for i, value in enumerate(values):
        rest = jnp.broadcast_to(value, (16, 128))
        for part in range(3):
            piece = rest.astype(BF16).astype(F32)
            block = jnp.where(row == 3 * i + part, piece, block)
            rest = rest - piece
    return block.astype(BF16)


def read_stat(block, i):
    return block[:, 3 * i : 3 * i + 1] + block[:, 3 * i + 1 : 3 * i + 2] + block[:, 3 * i + 2 : 3 * i + 3]


def pack(values):
    lane = lax.broadcasted_iota(jnp.int32, (1, 128), 1)
    block = jnp.zeros((1, 128), F32)
    for i, value in enumerate(values):
        block = jnp.where(lane == i, jnp.broadcast_to(value, (1, 128)), block)
    return block


def safe_divide(top, bottom):
    return jnp.where(bottom > 0, top / jnp.where(bottom > 0, bottom, 1.0), 0.0)


def drain(copies):
    for copy in copies:
        copy.wait_send()


def loop(count, body):
    def step(i, carry):
        body(i)
        return carry

    lax.fori_loop(0, count, step, 0)


def haydock_kernel(
    entries, factor,
    window_ref, dip_ref, energy_ref, cond_ref, val_ref, w_ref,
    out_ref,
    grid_ref, index_ref, perm_ref, cond_all, val_all, vv_ref, stage_ref, wt_ref,
    pack_ref, rows_ref, drow_ref, erow_ref, msg_ref, dips_ref, u_ref,
    half_ref, pair_ref, screen_ref, sum_ref, part_ref, first_ref, mine_ref, second_ref,
    after_ref, rests_ref, stat_ref, stats_ref, cut_ref,
    row_s, row_r, few_s, few_r, far_s, far_r, side_s, side_r, cond_s, cond_r, val_s, val_r, dip_s, dip_r, hop_s, hop_r, w_sem, own_sem,
    a_s, a_r, b_s, b_r, d_s, d_r, e_s, e_r,
):
    ka = lax.axis_index("ka")
    pb = lax.axis_index("pb")
    core = lax.rem(pb, 2)
    chip = pb // 2
    x = lax.rem(chip, 4)
    z = ka // 2
    side = lax.rem(ka, 2)
    y = chip // 4
    barrier = pltpu.get_barrier_semaphore()
    signal_all(barrier, ka, pb)
    mirror = {"ka": ka + 1 - 2 * side, "pb": lax.rem(pb + 8, N)}
    pl.semaphore_signal(barrier, inc=1, device_id=mirror, device_id_type=MESH)

    loads = [
        pltpu.make_async_copy(source, target, own_sem.at[1 + i])
        for i, (source, target) in enumerate(
            [
                (cond_ref, perm_ref.at[0]),
                (dip_ref, pack_ref.at[0]),
                (energy_ref, pack_ref.at[1]),
                (val_ref, val_all.at[pb]),
                (window_ref, grid_ref),
            ]
        )
    ]
    for load in loads:
        load.start()
    own_w = pltpu.make_async_copy(w_ref.at[:, :, core], stage_ref.at[pl.ds(core * 8, 8)], own_sem.at[0])
    own_w.start()
    to = lax.broadcasted_iota(jnp.int32, (64, 64), 0)
    fro = lax.broadcasted_iota(jnp.int32, (64, 64), 1)
    pick = (fro == 2 * lax.rem(to, 32) + to // 32).astype(F32).astype(BF16)
    for load in loads:
        load.wait()
    perm_ref[1] = jnp.dot(pick, perm_ref[0], preferred_element_type=F32).astype(BF16)
    cond_all[y, x, z, side] = perm_ref[1]
    rows_ref[pb] = pack_ref[...]
    def table(k):
        mine = grid_ref[k]
        for other in range(N):
            theirs = grid_ref[other]
            shift_one = jnp.bitwise_and(lax.shift_right_logical(mine, 5) - lax.shift_right_logical(theirs, 5), 3)
            shift_two = jnp.bitwise_and(lax.shift_right_logical(mine, 2) - lax.shift_right_logical(theirs, 2), 7)
            shift_three = jnp.bitwise_and(mine - theirs, 3)
            q = (shift_one * 8 + shift_two) * 4 + shift_three
            index_ref[k * N + other] = jnp.where(
                lax.shift_right_logical(q, 4) == chip, jnp.bitwise_and(q, 15), 16
            )

    loop(N, table)
    def turn(q):
        for j in range(8):
            wt_ref[j % 4, q, :, j // 4 * 128 : j // 4 * 128 + 128] = stage_ref[q, j].T

    own_w.wait()
    loop(8, lambda q: turn(core * 8 + q))
    for i in range(4):
        wt_ref[i, 16] = jnp.zeros((128, 256), BF16)
    pl.semaphore_wait(barrier, 2 * (N - 1) + 1)

    most = pl.ds(0, 48)
    few = pl.ds(48, 16)
    chips = [lax.rem(chip + o, 8) for o in range(1, 8)]

    def at(which):
        return {"pb": which * 2 + core}

    copies = [
        send_one(perm_ref.at[1, few], cond_all.at[y, x, z, side, few], few_s.at[o], few_r.at[chip], at(other))
        for o, other in enumerate(chips)
    ]
    copies += send_all(
        "ka", ka, lambda p: perm_ref.at[1, most], lambda p: cond_all.at[y, x, p // 2, lax.rem(p, 2), most], (cond_s, cond_r)
    )
    copies += send_all("pb", pb, lambda p: pack_ref, lambda p: rows_ref.at[p], (row_s, row_r))
    sibling = {"pb": pb + 1 - 2 * core}
    w_send = send_one(
        w_ref.at[:, :, 1 - core], stage_ref.at[pl.ds(core * 8, 8)], w_sem.at[0], w_sem.at[1], sibling
    )
    copies += [w_send]
    copies += send_all("pb", pb, lambda p: val_all.at[pb], lambda p: val_all.at[p], (val_s, val_r))

    parts = [lax.rem(x + o, 4) for o in (0, 3, 1, 2)]
    for o, other in enumerate(chips):
        recv_one(cond_all.at[other // 4, lax.rem(other, 4), z, side, few], few_s.at[o], few_r.at[other], at(other))

    beside = {"ka": ka + 1 - 2 * side}
    columns_z = [lax.rem(z + o, 8) for o in range(1, 8)]

    def send_far(part):
        block = cond_all.at[:, part, z, side, few]
        return [
            send_one(block, block, far_s.at[part, o], far_r.at[part, z], {"ka": other * 2 + side})
            for o, other in enumerate(columns_z)
        ]

    def pass_far(part):
        for o, other in enumerate(columns_z):
            block = cond_all.at[:, part, other, side, few]
            recv_one(block, far_s.at[part, o], far_r.at[part, other], {"ka": other * 2 + side})
        block = cond_all.at[:, part, :, side, few]
        return [send_one(block, block, side_s.at[part], side_r.at[part], beside)]

    for part in parts:
        copies += send_far(part)

    recv_all("ka", ka, lambda p: cond_all.at[y, x, p // 2, lax.rem(p, 2), most], (cond_s, cond_r))
    lower = pl.ds(0, 4)
    upper = pl.ds(4, 4)
    steps = [lax.rem(x + o, 4) for o in range(1, 4)]
    block = cond_all.at[y, x, :, :, most]
    copies += [send_one(block, block, hop_s.at[0], hop_r.at[0], mirror)]
    for o, slot, which in ((0, 1, upper), (2, 12, lower), (0, 10, lower), (2, 3, upper)):
        block = cond_all.at[y, x, which, :, most]
        copies += [send_one(block, block, hop_s.at[slot], hop_r.at[slot], at(y * 4 + steps[o]))]

    recv_all("pb", pb, lambda p: rows_ref.at[p], (row_s, row_r))
    for i in range(N):
        drow_ref[2 * i : 2 * i + 2, :] = rows_ref[i, 0]
        erow_ref[2 * i : 2 * i + 2, :] = rows_ref[i, 1]
    drow = drow_ref[...]
    msg_ref[0, 0:32, :] = drow.astype(BF16)
    msg_ref[0, 32:48, :] = stat_rows([total(drow * drow)])
    dips_ref[ka] = msg_ref[0]
    copies += send_all("ka", ka, lambda p: msg_ref.at[0], lambda p: dips_ref.at[p], (dip_s, dip_r))

    for o, slot, which, onward in ((0, 1, upper, 2), (2, 12, lower, 11)):
        near = steps[2 - o]
        block = cond_all.at[y, near, which, :, most]
        recv_one(block, hop_s.at[slot], hop_r.at[slot], at(y * 4 + near))
        copies += [send_one(block, block, hop_s.at[onward], hop_r.at[onward], at(y * 4 + steps[o]))]


    recv_one(stage_ref.at[pl.ds((1 - core) * 8, 8)], w_sem.at[0], w_sem.at[1], sibling)
    loop(8, lambda q: turn((1 - core) * 8 + q))

    for part in parts:
        copies += pass_far(part)
    recv_all("pb", pb, lambda p: val_all.at[p], (val_s, val_r))

    def spread(k):
        turned = val_all[k].T
        zero = jnp.zeros_like(turned)
        vv_ref[k] = jnp.concatenate(
            [jnp.concatenate([turned, zero], axis=1), jnp.concatenate([zero, turned], axis=1)], axis=0
        )

    for k in range(N):
        spread(k)
    recv_all("ka", ka, lambda p: dips_ref.at[p], (dip_s, dip_r))

    def start_apply(vector_ref):
        for k in range(N):
            both = lax.dot_general(vv_ref[k], vector_ref[k, 0:32, :], NT, preferred_element_type=F32)
            half_ref[k, :, 0:32] = both[0:128].astype(BF16)
            half_ref[k, :, 32:64] = both[128:256].astype(BF16)
            sum_ref[k] = jnp.zeros((64, 128), F32)

    def columns(part, k):
        return jnp.concatenate([cond_all[0, part, k // 2, k % 2], cond_all[1, part, k // 2, k % 2]], axis=1)

    def apply_part(part):
        def screen(g):
            for top in (0, 64):
                rows = slice(top, top + 64)
                accs = [jnp.zeros((64, 256), BF16)] * 4
                for other in range(N):
                    pair = pair_ref[other, rows, :]
                    for i in range(4):
                        accs[i] = accs[i] + wt_ref[part, index_ref[(g * 4 + i) * N + other], rows, :] * pair
                for i in range(4):
                    screen_ref[g * 4 + i, rows, :] = accs[i]

        for k in range(N):
            pair_ref[k] = jnp.dot(half_ref[k], columns(part, k), preferred_element_type=F32).astype(BF16)
        for g in range(N // 4):
            screen(g)
        for k in range(N):
            sum_ref[k] += lax.dot_general(columns(part, k), screen_ref[k], NT, preferred_element_type=F32)

    def finish_apply(which):
        for k in range(N):
            both = jnp.concatenate([sum_ref[k, 0:32, :], sum_ref[k, 32:64, :]], axis=1)
            high = both.astype(BF16)
            low = (both - high.astype(F32)).astype(BF16)
            part_ref[which, k] = (
                jnp.dot(high, vv_ref[k], preferred_element_type=F32)
                + jnp.dot(low, vv_ref[k], preferred_element_type=F32)
            ).astype(BF16)

    start_apply(dips_ref)
    recv_one(cond_all.at[1 - y, x, :, :, most], hop_s.at[0], hop_r.at[0], mirror)
    block = cond_all.at[1 - y, x, lower, :, most]
    for o in range(3):
        copies.append(send_one(block, block, hop_s.at[4 + o], hop_r.at[4 + o], at(y * 4 + steps[o])))

    def recv_far(part):
        recv_one(cond_all.at[:, part, :, 1 - side, few], side_s.at[part], side_r.at[part], beside)

    for i, o in enumerate((0, 2, 1)):
        near = parts[1 + i]
        if o != 0:
            recv_one(cond_all.at[y, near, upper, :, most], hop_s.at[1 + o], hop_r.at[1 + o], at(y * 4 + near))
        block = cond_all.at[y, near, upper, :, most]
        copies.append(send_one(block, block, hop_s.at[7 + o], hop_r.at[7 + o], mirror))
    recv_far(parts[0])
    apply_part(parts[0])
    for i, o in enumerate((0, 2, 1)):
        near = parts[1 + i]
        if o != 2:
            recv_one(cond_all.at[y, near, lower, :, most], hop_s.at[10 + o], hop_r.at[10 + o], at(y * 4 + near))
        recv_one(cond_all.at[1 - y, near, lower, :, most], hop_s.at[4 + o], hop_r.at[4 + o], at(y * 4 + near))
        recv_one(cond_all.at[1 - y, near, upper, :, most], hop_s.at[7 + o], hop_r.at[7 + o], mirror)
        recv_far(near)
        apply_part(near)
    finish_apply(0)

    def reduce_rows(which, before):
        new = send_all(
            "ka", ka, lambda p: part_ref.at[which, p], lambda p: first_ref.at[which, p], (a_s.at[which], a_r.at[which])
        )
        first_ref[which, ka] = part_ref[which, ka]
        drain(before)
        recv_all("ka", ka, lambda p: first_ref.at[which, p], (a_s.at[which], a_r.at[which]))
        mine_ref[which] = jnp.sum(first_ref[which].astype(F32), axis=0).astype(BF16)
        second_ref[which, pb] = mine_ref[which]
        last = send_all(
            "pb", pb, lambda p: mine_ref.at[which], lambda p: second_ref.at[which, p], (b_s.at[which], b_r.at[which])
        )
        drain(new)
        recv_all("pb", pb, lambda p: second_ref.at[which, p], (b_s.at[which], b_r.at[which]))
        return jnp.sum(second_ref[which].astype(F32), axis=0), last

    kernel_row, copies = reduce_rows(0, copies)
    squares = read_stat(dips_ref[:, 32:48, :].astype(F32), 0)
    scale = 1.0 / jnp.sqrt(jnp.sum(squares, axis=0) / entries + EPSILON)
    vector = drow_ref[...] * scale
    image = erow_ref[...] * vector - factor * scale * kernel_row
    norm = total(vector * vector)
    inner = total(vector * image)
    slope = safe_divide(inner, norm)
    rest = image - slope * vector
    msg_ref[1, 0:32, :] = rest.astype(BF16)
    msg_ref[1, 32:48, :] = stat_rows([inner, slope, total(rest * rest), norm])
    rests_ref[ka] = msg_ref[1]
    copies += send_all("ka", ka, lambda p: msg_ref.at[1], lambda p: rests_ref.at[p], (d_s, d_r))
    recv_all("ka", ka, lambda p: rests_ref.at[p], (d_s, d_r))
    stats = rests_ref[:, 32:48, :].astype(F32)
    alpha_zero = jnp.sum(read_stat(stats, 0), axis=0) / entries
    off = read_stat(stats, 1) - alpha_zero
    square = jnp.sum(read_stat(stats, 2) + read_stat(stats, 3) * off * off, axis=0) / entries
    beta_zero = jnp.sqrt(square + EPSILON)
    scaled = off * scale
    for k in range(N):
        u_ref[k] = (
            rests_ref[k, 0:32, :].astype(F32) + scaled[k] * dips_ref[k, 0:32, :].astype(F32)
        ).astype(BF16)
    after_ref[0] = vector
    after_ref[1] = (image - alpha_zero * vector) / beta_zero

    start_apply(u_ref)
    for part in range(4):
        apply_part(part)
    finish_apply(1)
    kernel_row, copies = reduce_rows(1, copies)
    former = after_ref[0]
    vector = after_ref[1]
    image = erow_ref[...] * vector - factor / beta_zero * kernel_row
    rest = image - beta_zero * former
    norm = total(vector * vector)
    slope = safe_divide(total(vector * rest), norm)
    gap = rest - slope * vector
    stat_ref[...] = pack([total(vector * image), slope, total(gap * gap), norm])
    stats_ref[ka] = stat_ref[...]
    final = send_all("ka", ka, lambda p: stat_ref, lambda p: stats_ref.at[p], (e_s, e_r))
    drain(copies)
    recv_all("ka", ka, lambda p: stats_ref.at[p], (e_s, e_r))
    stats = stats_ref[...]
    inners, slopes, lefts, norms = [
        jnp.broadcast_to(stats[:, :, i : i + 1], (N, 1, 128)) for i in range(4)
    ]
    alpha = jnp.sum(inners, axis=0) / entries
    off = slopes - alpha
    beta = jnp.sqrt(jnp.sum(lefts + norms * off * off, axis=0) / entries + EPSILON)
    last = (rest - alpha * vector) / beta
    for i in range(N):
        cut_ref[i] = last[2 * i : 2 * i + 2, :]
    out_ref[0:2, :] = cut_ref[pb]
    lane = lax.broadcasted_iota(jnp.int32, (1, 128), 1)
    out_ref[2:3, :] = jnp.where(
        lane == 0, alpha_zero, jnp.where(lane == 1, alpha, jnp.where(lane == 2, beta_zero, beta))
    )
    drain(final)


def haydock(entries, factor, *args):
    sem = pltpu.SemaphoreType.DMA
    vmem = pl.BlockSpec(memory_space=pltpu.VMEM)
    pair = [sem((N,)), sem((N,))]
    return pl.pallas_call(
        functools.partial(haydock_kernel, entries, factor),
        out_shape=jax.ShapeDtypeStruct((3, 128), F32),
        in_specs=[pl.BlockSpec(memory_space=pltpu.HBM)] * 6,
        out_specs=vmem,
        scratch_shapes=[
            pltpu.SMEM((N,), jnp.int32),
            pltpu.SMEM((N * N,), jnp.int32),
            pltpu.VMEM((2, 64, 128), BF16),
            pltpu.VMEM((2, 4, 8, 2, 64, 128), BF16),
            pltpu.VMEM((N, 64, 128), BF16),
            pltpu.VMEM((N, 256, 128), BF16),
            pltpu.VMEM((16, 8, 128, 128), BF16),
            pltpu.VMEM((4, 17, 128, 256), BF16),
            pltpu.VMEM((2, 2, 128), F32),
            pltpu.VMEM((N, 2, 2, 128), F32),
            pltpu.VMEM((32, 128), F32),
            pltpu.VMEM((32, 128), F32),
            pltpu.VMEM((2, 48, 128), BF16),
            pltpu.VMEM((N, 48, 128), BF16),
            pltpu.VMEM((N, 32, 128), BF16),
            pltpu.VMEM((N, 128, 64), BF16),
            pltpu.VMEM((N, 128, 256), BF16),
            pltpu.VMEM((N, 128, 256), BF16),
            pltpu.VMEM((N, 64, 128), F32),
            pltpu.VMEM((2, N, 32, 128), BF16),
            pltpu.VMEM((2, N, 32, 128), BF16),
            pltpu.VMEM((2, 32, 128), BF16),
            pltpu.VMEM((2, N, 32, 128), BF16),
            pltpu.VMEM((2, 32, 128), F32),
            pltpu.VMEM((N, 48, 128), BF16),
            pltpu.VMEM((1, 128), F32),
            pltpu.VMEM((N, 1, 128), F32),
            pltpu.VMEM((N, 2, 128), F32),
        ]
        + pair * 2
        + [sem((4, N)), sem((4, N)), sem((4,)), sem((4,))]
        + pair * 4
        + [sem((2,)), sem((6,))]
        + [sem((2, N))] * 4
        + pair * 2,
        compiler_params=pltpu.CompilerParams(
            collective_id=0, has_side_effects=True, vmem_limit_bytes=63 * 1024 * 1024
        ),
        name="haydock",
    )(*args)


def per_device(dipole, energy, cond_amp, val_amp, screened, window):
    entries = 16 * 4096
    factor = 1.0 / (2048 * math.sqrt(entries))
    out = haydock(
        entries,
        factor,
        window,
        dipole.reshape(2, 128),
        energy.reshape(2, 128),
        cond_amp[0],
        val_amp[0],
        screened.reshape(8, 8, 2, 128, 128),
    )
    return out[2, :4], out[:2].reshape(1, 256)


def solution(mesh):
    in_specs = (
        P("ka", "pb"),
        P("ka", "pb"),
        P("ka", None, "pb"),
        P("pb", None, "ka"),
        P("pb", None, "ka"),
        P(),
    )
    out_specs = (P(), P("ka", "pb"))
    return jax.shard_map(
        per_device, mesh=mesh, in_specs=in_specs, out_specs=out_specs, check_vma=False
    )
```
